512 devices in a mesh: dp: 32 (over x, y), fsdp: 16 (over z, core).
Axes of the slice: x: 4, y: 8, z: 8, core: 2. Of those that a mesh axis runs over, the one named last changes fastest.
Arguments:
- grad_parts: float32 [32, 16, 16, 28672], P('dp', 'fsdp'), may hold values from -6 to 6
- momentum: float32 [32, 16, 28672], P('dp', 'fsdp'), may hold values from -24 to 24
- positions: int32 [32, 16, 4, 448], P(None, 'fsdp'), may hold values from 0 to 63, as said below
Outputs:
- update: float32 [16, 28672], P('fsdp')
- new_momentum: float32 [32, 16, 28672], P('dp', 'fsdp')
The draws below stay inside these ranges and needn't reach their ends.
Inputs may be any that keep to these rules, and one draw needn't show every extreme that they name: For every replica, row and block the 4 positions are different.
All inputs are finite; a program needn't handle non-finite values.
Results may differ from the reference program's by a relative error of at most 0.0003.
Values sent between devices are 32-bit elements; how exact they have to be, the bound alone decides.
No kernel may reach another device: no remote copies, remote signals or barrier semaphores. Data moves between devices by JAX's collectives and lax.ppermute only.
A program may use at most 64 MiB of HBM per device.

```python
import jax
import jax.numpy as jnp
from jax import lax

F = 28672
KEEP = 4
ROWS = 16
SPANS = 448
REPLICAS = 32
N_FSDP = 16


def draw_positions(key, part):
    key = jax.random.fold_in(key, 7)
    scores = jax.random.randint(key, (REPLICAS, ROWS, SPANS, 64), 0, 1 << 20, dtype=jnp.int32)
    scores = scores * 64 + jnp.arange(64, dtype=jnp.int32)
    ignored, chosen = lax.top_k(scores, KEEP)
    return jnp.transpose(chosen.astype(jnp.int32), (0, 1, 3, 2))


def with_spikes(result, own_key, source, target, blocks, factor):
    def block_of(axis_at):
        return (jnp.arange(result.shape[axis_at]) // (result.shape[axis_at] // blocks)).reshape((-1,) + (1,) * (result.ndim - 1 - axis_at))

    near = jax.random.permutation(own_key, blocks)[block_of(target)]
    second = (block_of(target) + blocks // 2) % blocks
    return jnp.where((block_of(source) == near) | (block_of(source) == second), factor * result, result)


def steps_of(rng, shape, cuts, smallest, largest):
    factor_of, own = 1.0, jax.random.fold_in(rng, 6)
    for position, parts in cuts:
        draws = jnp.exp(jax.random.uniform(jax.random.fold_in(own, position), (parts,), jnp.float32, smallest / len(cuts), largest / len(cuts)))
        factor_of = factor_of * jnp.repeat(draws, shape[position] // parts).reshape([-1 if axis == position else 1 for axis in range(len(shape))])
    return factor_of


def bell_draw(stream_key, shape, scale, bound, cuts=(), kind=jnp.bfloat16):
    drawn = scale * jax.random.normal(stream_key, shape, jnp.float32)
    if cuts:
        drawn = drawn * steps_of(stream_key, shape, cuts, -0.22, 0.18)
    return jnp.clip(drawn, -bound, bound).astype(kind)


def bell_draw_with(key, shape, spread, reach, cuts, heavy, kind=jnp.bfloat16):
    values = spread * jax.random.normal(key, shape, jnp.float32)
    if cuts:
        values = values * steps_of(key, shape, cuts, -0.22, 0.18)
    return jnp.clip(with_spikes(values, jax.random.fold_in(key, 3), *heavy), -reach, reach).astype(kind)


def setup_inputs(seed: int = 0) -> dict:
    key_list = jax.random.split(jax.random.key(seed), 4)
    grad_parts = bell_draw_with(key_list[0], (REPLICAS, N_FSDP, ROWS, F), 1.0, 6.0, ((0, 32), (1, 16)), (1, 2, 16, 2.0), jnp.float32)
    momentum = bell_draw(key_list[1], (REPLICAS, ROWS, F), 4.0, 24.0, ((0, 32), (1, 16)), jnp.float32)
    positions = draw_positions(jax.random.fold_in(key_list[3], 71), 0)
    return {"grad_parts": grad_parts, "momentum": momentum, "positions": positions}


decay_rate = 0.999
epsilon = 1e-06

def cosine_table():
    levels = jnp.arange(64, dtype=jnp.float32)
    frequency = levels[:, None]
    sample = levels[None, :]
    cosines = jnp.cos(jnp.pi * (2.0 * sample + 1.0) * frequency / 128.0)
    norming = jnp.where(frequency == 0.0, jnp.sqrt(1.0 / 64.0), jnp.sqrt(2.0 / 64.0))
    return cosines * norming

def reference(grad_parts, momentum, positions):
    cosines = cosine_table()

    def per_replica(running, inputs):
        partials, moment, places = inputs
        gradient = lax.optimization_barrier(jnp.sum(partials, axis=0))
        accumulated = decay_rate * moment + gradient
        blocks = accumulated.reshape(ROWS, SPANS, 64)
        coeffs = jnp.einsum('rcn,kn->rck', blocks, cosines, precision=lax.Precision.HIGHEST)
        ordered = jnp.transpose(places, (0, 2, 1)).astype(jnp.int32)
        kept_values = jnp.take_along_axis(coeffs, ordered, axis=2)
        one_hot = ordered[..., None] == jnp.arange(64, dtype=jnp.int32)
        dense_coeffs = lax.optimization_barrier(jnp.sum(jnp.where(one_hot, kept_values[..., None], 0.0), axis=2))
        removed = jnp.einsum('rck,kn->rcn', dense_coeffs, cosines, precision=lax.Precision.HIGHEST)
        new_moment = accumulated - removed.reshape(ROWS, F)
        return (running + dense_coeffs, new_moment)
    empty_sum = jnp.zeros((ROWS, SPANS, 64), jnp.float32)
    summed, new_momentum = lax.scan(per_replica, empty_sum, (grad_parts, momentum, positions))
    averaged = jnp.einsum('rck,kn->rcn', summed, cosines, precision=lax.Precision.HIGHEST) / REPLICAS
    meansq = lax.optimization_barrier(jnp.mean(averaged * averaged, axis=-1, keepdims=True))
    update = averaged / jnp.sqrt(averaged * averaged + meansq + epsilon)
    return (update.reshape(ROWS, F), new_momentum)
```

```python
import functools

import jax
import jax.numpy as jnp
import numpy as np
from jax import lax
from jax.experimental import pallas as pl
from jax.experimental.pallas import tpu as pltpu
from jax.sharding import PartitionSpec as P

decay_rate = 0.999
epsilon = 1e-06
block = 64
lanes = 128
keep = 4
f32, bf16 = jnp.float32, jnp.bfloat16


def paired_table():
    frequency = np.arange(block)[:, None]
    sample = np.arange(block)[None, :]
    cosines = np.cos(np.pi * (2.0 * sample + 1.0) * frequency / (2.0 * block))
    norming = np.where(frequency == 0, np.sqrt(1.0 / block), np.sqrt(2.0 / block))
    return np.kron(np.eye(2), cosines * norming).astype(np.float32)


def split_table():
    table = paired_table()
    high = table.astype(jnp.bfloat16)
    low = (table - high.astype(np.float32)).astype(jnp.bfloat16)
    return np.stack([high, low])


def halves(x):
    high = x.astype(bf16)
    return high, (x - high.astype(f32)).astype(bf16)


def dot3(x, table_ref, dims, table_first):
    high, low = halves(x)

    def one(part, index):
        pair = (table_ref[index], part) if table_first else (part, table_ref[index])
        return lax.dot_general(*pair, (dims, ((), ())), preferred_element_type=f32)

    return one(high, 0) + (one(low, 0) + one(high, 1))


def forward(fields, table_ref):
    return dot3(fields, table_ref, ((1,), (1,)), True)


def inverse(coeffs, table_ref):
    return dot3(coeffs, table_ref, ((0,), (0,)), False)


def same_core_rows(x, odd):
    upper, lower = x[:8], x[8:]
    row = lax.broadcasted_iota(jnp.int32, upper.shape, 0)
    even_place = row % 2 == 0
    return jnp.where(
        odd,
        jnp.where(even_place, pltpu.roll(upper, 7, 0), lower),
        jnp.where(even_place, upper, pltpu.roll(lower, 1, 0)),
    )


def pack_kernel(other, odd_ref, grad_ref, out_ref, mixed):
    tiles = out_ref.shape[1]
    odd = (odd_ref[0] != 0) != other
    for tile in range(tiles):
        mixed[8 * tile : 8 * tile + 8, :] = same_core_rows(
            grad_ref[:, tile * lanes : (tile + 1) * lanes], odd
        )
    for place in range(8):
        out_ref[place // 2 + 4 * (place % 2)] = mixed[pl.ds(place, tiles, stride=8), :]


def pack(grad, odd, other):
    rows, columns = grad.shape
    tiles = columns // lanes
    steps = 4
    step_tiles = tiles // steps
    return pl.pallas_call(
        functools.partial(pack_kernel, other),
        grid=(steps,),
        in_specs=[
            pl.BlockSpec(memory_space=pltpu.SMEM),
            pl.BlockSpec((rows, step_tiles * lanes), lambda i: (0, i)),
        ],
        out_specs=pl.BlockSpec((rows // 2, step_tiles, lanes), lambda i: (0, i, 0)),
        out_shape=jax.ShapeDtypeStruct((rows // 2, tiles, lanes), f32),
        scratch_shapes=[pltpu.VMEM((8 * step_tiles, lanes), f32)],
        cost_estimate=pl.CostEstimate(flops=rows * columns, bytes_accessed=6 * rows * columns, transcendentals=0),
        name="pack_other" if other else "pack_own",
    )(odd, grad)


def places_kernel(places_ref, out_ref):
    replicas, count, spans = places_ref.shape
    half = spans // 2
    source = lax.broadcasted_iota(jnp.int32, (spans, half), 0)
    target = lax.broadcasted_iota(jnp.int32, (spans, half), 1)
    places = places_ref[...].reshape(replicas * count, spans).astype(f32).astype(bf16)
    for parity in range(2):
        chooser = (source == 2 * target + parity).astype(f32).astype(bf16)
        chosen = jnp.dot(places, chooser, preferred_element_type=f32)
        out_ref[:, parity * count : (parity + 1) * count, :] = chosen.reshape(replicas, count, half)


def split_places(positions):
    replicas, count, spans = positions.shape
    return pl.pallas_call(
        places_kernel,
        out_shape=jax.ShapeDtypeStruct((replicas, 2 * count, spans // 2), f32),
        cost_estimate=pl.CostEstimate(flops=2 * replicas * count * spans * spans, bytes_accessed=8 * replicas * count * spans, transcendentals=0),
        name="split_places",
    )(positions)


def moment_kernel(me_ref, parts_ref, moment_ref, places_ref, table_ref, kept_ref, new_ref):
    accumulated = decay_rate * moment_ref[...]
    gradient = parts_ref[0]
    for source in range(1, parts_ref.shape[0]):
        gradient = gradient + parts_ref[source]
    accumulated = accumulated + gradient
    coeffs = forward(accumulated, table_ref)
    half = coeffs.shape[1]
    level = lax.broadcasted_iota(jnp.int32, (block, half), 0).astype(f32)
    own = places_ref[me_ref[0]]
    dense = []
    for parity in range(2):
        mine = coeffs[parity * block : (parity + 1) * block]
        inside = jnp.zeros_like(mine)
        for j in range(keep):
            row = parity * keep + j
            picked = jnp.where(own[row : row + 1] == level, mine, 0.0)
            inside = inside + picked
            kept_ref[row : row + 1, :] = jnp.sum(picked, axis=0, keepdims=True)
        dense.append(inside)
    new_ref[...] = accumulated - inverse(jnp.concatenate(dense, axis=0), table_ref)


def moment_step(me, parts, moment, places, table):
    sources, tiles, width = parts.shape
    whole = pl.BlockSpec(memory_space=pltpu.VMEM)
    return pl.pallas_call(
        moment_kernel,
        in_specs=[pl.BlockSpec(memory_space=pltpu.SMEM), whole, whole, whole, whole],
        out_specs=[whole, whole],
        out_shape=[
            jax.ShapeDtypeStruct((2 * keep, tiles), f32),
            jax.ShapeDtypeStruct((tiles, width), f32),
        ],
        cost_estimate=pl.CostEstimate(flops=12 * tiles * width * width, bytes_accessed=4 * (sources + 2) * tiles * width, transcendentals=0),
        name="moment_step",
    )(me, parts, moment, places, table)


def update_kernel(kept_ref, places_ref, table_ref, out_ref):
    replicas, _, half = kept_ref.shape
    level = lax.broadcasted_iota(jnp.int32, (block, half), 0).astype(f32)

    def one_replica(r, sums):
        values, places = kept_ref[r], places_ref[r]
        added = []
        for parity in range(2):
            dense = jnp.zeros((block, half), f32)
            for j in range(keep):
                row = parity * keep + j
                dense = jnp.where(places[row : row + 1] == level, values[row : row + 1], dense)
            added.append(sums[parity] + dense)
        return tuple(added)

    empty = jnp.zeros((block, half), f32)
    sums = lax.fori_loop(0, replicas, one_replica, (empty, empty), unroll=2)
    averaged = inverse(jnp.concatenate(sums, axis=0), table_ref) * (1.0 / replicas)
    squares = averaged * averaged
    high, low = halves(squares)
    row = lax.broadcasted_iota(jnp.int32, (lanes, lanes), 0) // block
    column = lax.broadcasted_iota(jnp.int32, (lanes, lanes), 1) // block
    same = (row == column).astype(f32).astype(bf16)
    meansq = jnp.dot(high, same, preferred_element_type=f32) + jnp.dot(low, same, preferred_element_type=f32)
    out_ref[...] = averaged * lax.rsqrt(squares + meansq * (1.0 / block) + epsilon)


def update_step(kept, places, table):
    replicas, _, half = kept.shape
    return pl.pallas_call(
        update_kernel,
        out_shape=jax.ShapeDtypeStruct((half, lanes), f32),
        cost_estimate=pl.CostEstimate(flops=9 * replicas * lanes * half, bytes_accessed=8 * kept.size, transcendentals=lanes * half),
        name="update_step",
    )(kept, places, table)


def body(grad_parts, momentum, positions):
    columns = momentum.shape[-1]
    tiles = columns // lanes
    devices = lax.axis_size("fsdp")
    replicas = lax.axis_size("dp")
    me = lax.axis_index("fsdp")
    odd = (me % 2).reshape(1)
    grad = grad_parts[0, 0]
    table = jnp.asarray(split_table())
    sent = pack(grad, odd, True)
    arrived = lax.ppermute(sent, "fsdp", [(i, i ^ 1) for i in range(devices)])
    own = pack(grad, odd, False)
    places = split_places(positions[:, 0])
    groups = [list(range(core, devices, 2)) for core in range(2)]
    parts = lax.all_to_all(own + arrived, "fsdp", 0, 0, tiled=True, axis_index_groups=groups)
    kept, new_moment = moment_step(
        lax.axis_index("dp").reshape(1), parts, momentum.reshape(tiles, lanes), places, table
    )
    everyone = lax.all_to_all(
        jnp.broadcast_to(kept[None], (replicas,) + kept.shape), "dp", 0, 0, tiled=True
    )
    update = update_step(everyone, places, table)
    return update.reshape(1, columns), new_moment.reshape(1, 1, columns)


def solution(mesh):
    in_specs = (P("dp", "fsdp", None, None), P("dp", "fsdp", None), P(None, "fsdp", None, None))
    out_specs = (P("fsdp", None), P("dp", "fsdp", None))
    return jax.shard_map(body, mesh=mesh, in_specs=in_specs, out_specs=out_specs, check_vma=False)
```

```python
import functools

import jax
import jax.numpy as jnp
import numpy as np
from jax import lax
from jax.experimental import pallas as pl
from jax.experimental.pallas import tpu as pltpu
from jax.sharding import PartitionSpec as P

decay_rate = 0.999
epsilon = 1e-06
block = 64
lanes = 128
keep = 4
f32, bf16 = jnp.float32, jnp.bfloat16
whole = pl.BlockSpec(memory_space=pltpu.VMEM)
params = pltpu.CompilerParams(vmem_limit_bytes=12 * 2**20)


def paired_table():
    frequency = np.arange(block)[:, None]
    sample = np.arange(block)[None, :]
    cosines = np.cos(np.pi * (2.0 * sample + 1.0) * frequency / (2.0 * block))
    norming = np.where(frequency == 0, np.sqrt(1.0 / block), np.sqrt(2.0 / block))
    return np.kron(np.eye(2), cosines * norming).astype(np.float32)


def split_table():
    table = paired_table()
    high = table.astype(jnp.bfloat16)
    low = (table - high.astype(np.float32)).astype(jnp.bfloat16)
    return np.stack([high, low])


def halves(x):
    high = x.astype(bf16)
    return high, (x - high.astype(f32)).astype(bf16)


def dot3(x, table_ref, dims, table_first):
    high, low = halves(x)

    def one(part, index):
        pair = (table_ref[index], part) if table_first else (part, table_ref[index])
        return lax.dot_general(*pair, (dims, ((), ())), preferred_element_type=f32)

    return one(high, 0) + (one(low, 0) + one(high, 1))


def forward(fields, table_ref):
    return dot3(fields, table_ref, ((1,), (1,)), True)


def inverse(coeffs, table_ref):
    return dot3(coeffs, table_ref, ((0,), (0,)), False)


def same_core_rows(x, odd):
    upper, lower = x[:8], x[8:]
    row = lax.broadcasted_iota(jnp.int32, upper.shape, 0)
    even_place = row % 2 == 0
    return jnp.where(
        odd,
        jnp.where(even_place, pltpu.roll(upper, 7, 0), lower),
        jnp.where(even_place, upper, pltpu.roll(lower, 1, 0)),
    )


def pack_kernel(other, odd_ref, grad_ref, out_ref):
    odd = (odd_ref[0] != 0) != other
    for first in range(0, out_ref.shape[1], 8):
        mixed = jnp.stack(
            [
                same_core_rows(grad_ref[:, tile * lanes : (tile + 1) * lanes], odd)
                for tile in range(first, first + 8)
            ]
        )
        rows = jnp.swapaxes(mixed, 0, 1)
        for place in range(8):
            out_ref[place // 2 + 4 * (place % 2), first : first + 8, :] = rows[place]


def pack(grad, odd, other):
    rows, columns = grad.shape
    return pl.pallas_call(
        functools.partial(pack_kernel, other),
        in_specs=[pl.BlockSpec(memory_space=pltpu.SMEM), whole],
        out_specs=whole,
        out_shape=jax.ShapeDtypeStruct((rows // 2, columns // lanes, lanes), f32),
        compiler_params=params,
        cost_estimate=pl.CostEstimate(flops=rows * columns, bytes_accessed=6 * rows * columns, transcendentals=0),
        name="pack_other" if other else "pack_own",
    )(odd, grad)


def places_kernel(places_ref, out_ref):
    replicas, count, spans = places_ref.shape
    half = spans // 2
    source = lax.broadcasted_iota(jnp.int32, (spans, half), 0)
    target = lax.broadcasted_iota(jnp.int32, (spans, half), 1)
    places = places_ref[...].reshape(replicas * count, spans).astype(f32).astype(bf16)
    for parity in range(2):
        chooser = (source == 2 * target + parity).astype(f32).astype(bf16)
        chosen = jnp.dot(places, chooser, preferred_element_type=f32)
        out_ref[:, parity * count : (parity + 1) * count, :] = chosen.reshape(replicas, count, half)


def split_places(positions):
    replicas, count, spans = positions.shape
    return pl.pallas_call(
        places_kernel,
        out_shape=jax.ShapeDtypeStruct((replicas, 2 * count, spans // 2), f32),
        in_specs=[whole],
        out_specs=whole,
        compiler_params=params,
        cost_estimate=pl.CostEstimate(flops=2 * replicas * count * spans * spans, bytes_accessed=8 * replicas * count * spans, transcendentals=0),
        name="split_places",
    )(positions)


def moment_kernel(me_ref, parts_ref, moment_ref, places_ref, table_ref, kept_ref, new_ref):
    accumulated = decay_rate * moment_ref[...]
    gradient = parts_ref[0]
    for source in range(1, parts_ref.shape[0]):
        gradient = gradient + parts_ref[source]
    accumulated = accumulated + gradient
    coeffs = forward(accumulated, table_ref)
    half = coeffs.shape[1]
    level = lax.broadcasted_iota(jnp.int32, (block, half), 0).astype(f32)
    own = places_ref[me_ref[0]]
    dense, kept = [], []
    for parity in range(2):
        mine = coeffs[parity * block : (parity + 1) * block]
        inside = jnp.zeros_like(mine)
        for j in range(keep):
            row = parity * keep + j
            picked = jnp.where(own[row : row + 1] == level, mine, 0.0)
            inside = inside + picked
            kept.append(jnp.sum(picked, axis=0, keepdims=True))
        dense.append(inside)
    kept_ref[...] = jnp.broadcast_to(jnp.concatenate(kept, axis=0)[None], kept_ref.shape)
    new_ref[...] = accumulated - inverse(jnp.concatenate(dense, axis=0), table_ref)


def moment_step(me, parts, moment, places, table):
    replicas = places.shape[0]
    sources, tiles, width = parts.shape
    return pl.pallas_call(
        moment_kernel,
        in_specs=[pl.BlockSpec(memory_space=pltpu.SMEM), whole, whole, whole, whole],
        out_specs=[whole, whole],
        out_shape=[
            jax.ShapeDtypeStruct((replicas, 2 * keep, tiles), f32),
            jax.ShapeDtypeStruct((tiles, width), f32),
        ],
        compiler_params=params,
        cost_estimate=pl.CostEstimate(flops=12 * tiles * width * width, bytes_accessed=4 * (sources + 2) * tiles * width, transcendentals=0),
        name="moment_step",
    )(me, parts, moment, places, table)


def update_kernel(kept_ref, places_ref, table_ref, out_ref):
    replicas, _, half = kept_ref.shape
    sums = []
    for parity in range(2):
        columns = []
        for first in range(0, half, lanes):
            at = slice(first, min(first + lanes, half))
            level = lax.broadcasted_iota(jnp.int32, (block, at.stop - first), 0).astype(f32)

            def one_replica(r, total):
                dense = jnp.zeros(level.shape, f32)
                for j in range(keep):
                    row = pl.ds(parity * keep + j, 1)
                    dense = jnp.where(places_ref[r, row, at] == level, kept_ref[r, row, at], dense)
                return total + dense

            columns.append(lax.fori_loop(0, replicas, one_replica, jnp.zeros(level.shape, f32), unroll=4))
        sums.append(jnp.concatenate(columns, axis=1))
    averaged = inverse(jnp.concatenate(sums, axis=0), table_ref) * (1.0 / replicas)
    squares = averaged * averaged
    high, low = halves(squares)
    row = lax.broadcasted_iota(jnp.int32, (lanes, lanes), 0) // block
    column = lax.broadcasted_iota(jnp.int32, (lanes, lanes), 1) // block
    same = (row == column).astype(f32).astype(bf16)
    meansq = jnp.dot(high, same, preferred_element_type=f32) + jnp.dot(low, same, preferred_element_type=f32)
    out_ref[...] = averaged * lax.rsqrt(squares + meansq * (1.0 / block) + epsilon)


def update_step(kept, places, table):
    replicas, _, half = kept.shape
    return pl.pallas_call(
        update_kernel,
        out_shape=jax.ShapeDtypeStruct((half, lanes), f32),
        in_specs=[whole] * 3,
        out_specs=whole,
        compiler_params=params,
        cost_estimate=pl.CostEstimate(flops=9 * replicas * lanes * half, bytes_accessed=8 * kept.size, transcendentals=lanes * half),
        name="update_step",
    )(kept, places, table)


def body(grad_parts, momentum, positions):
    columns = momentum.shape[-1]
    tiles = columns // lanes
    devices = lax.axis_size("fsdp")
    me = lax.axis_index("fsdp")
    odd = (me % 2).reshape(1)
    grad = grad_parts[0, 0]
    table = jnp.asarray(split_table())
    sent = pack(grad, odd, True)
    arrived = lax.ppermute(sent, "fsdp", [(i, i ^ 1) for i in range(devices)])
    own = pack(grad, odd, False)
    places = split_places(positions[:, 0])
    groups = [list(range(core, devices, 2)) for core in range(2)]
    parts = lax.all_to_all(own + arrived, "fsdp", 0, 0, tiled=True, axis_index_groups=groups)
    kept, new_moment = moment_step(
        lax.axis_index("dp").reshape(1), parts, momentum.reshape(tiles, lanes), places, table
    )
    everyone = lax.all_to_all(kept, "dp", 0, 0, tiled=True)
    update = update_step(everyone, places, table)
    return update.reshape(1, columns), new_moment.reshape(1, 1, columns)


def solution(mesh):
    in_specs = (P("dp", "fsdp", None, None), P("dp", "fsdp", None), P(None, "fsdp", None, None))
    out_specs = (P("fsdp", None), P("dp", "fsdp", None))
    return jax.shard_map(body, mesh=mesh, in_specs=in_specs, out_specs=out_specs, check_vma=False)
```

```python
import functools

import jax
import jax.numpy as jnp
import numpy as np
from jax import lax
from jax.experimental import pallas as pl
from jax.experimental.pallas import tpu as pltpu
from jax.sharding import PartitionSpec as P

decay_rate = 0.999
epsilon = 1e-06
block = 64
lanes = 128
keep = 4
f32, bf16 = jnp.float32, jnp.bfloat16
whole = pl.BlockSpec(memory_space=pltpu.VMEM)
params = pltpu.CompilerParams(vmem_limit_bytes=12 * 2**20)


def paired_table():
    frequency = np.arange(block)[:, None]
    sample = np.arange(block)[None, :]
    cosines = np.cos(np.pi * (2.0 * sample + 1.0) * frequency / (2.0 * block))
    norming = np.where(frequency == 0, np.sqrt(1.0 / block), np.sqrt(2.0 / block))
    return np.kron(np.eye(2), cosines * norming).astype(np.float32)


def split_table():
    table = paired_table()
    high = table.astype(jnp.bfloat16)
    low = (table - high.astype(np.float32)).astype(jnp.bfloat16)
    return np.stack([high, low])


def halves(x):
    high = x.astype(bf16)
    return high, (x - high.astype(f32)).astype(bf16)


def dot3(x, table_ref, dims, table_first):
    high, low = halves(x)

    def one(part, index):
        pair = (table_ref[index], part) if table_first else (part, table_ref[index])
        return lax.dot_general(*pair, (dims, ((), ())), preferred_element_type=f32)

    return one(high, 0) + (one(low, 0) + one(high, 1))


def forward(fields, table_ref):
    return dot3(fields, table_ref, ((1,), (1,)), True)


def inverse(coeffs, table_ref):
    return dot3(coeffs, table_ref, ((0,), (0,)), False)


def same_core_rows(x, odd):
    upper, lower = x[:8], x[8:]
    row = lax.broadcasted_iota(jnp.int32, upper.shape, 0)
    even_place = row % 2 == 0
    return jnp.where(
        odd,
        jnp.where(even_place, pltpu.roll(upper, 7, 0), lower),
        jnp.where(even_place, upper, pltpu.roll(lower, 1, 0)),
    )


def pack_kernel(other, odd_ref, grad_ref, out_ref):
    odd = (odd_ref[0] != 0) != other
    for first in range(0, out_ref.shape[1], 8):
        mixed = jnp.stack(
            [
                same_core_rows(grad_ref[:, tile * lanes : (tile + 1) * lanes], odd)
                for tile in range(first, first + 8)
            ]
        )
        rows = jnp.swapaxes(mixed, 0, 1)
        for place in range(8):
            out_ref[place // 2 + 4 * (place % 2), first : first + 8, :] = rows[place]


def pack(grad, odd, other):
    rows, columns = grad.shape
    return pl.pallas_call(
        functools.partial(pack_kernel, other),
        in_specs=[pl.BlockSpec(memory_space=pltpu.SMEM), whole],
        out_specs=whole,
        out_shape=jax.ShapeDtypeStruct((rows // 2, columns // lanes, lanes), f32),
        compiler_params=params,
        cost_estimate=pl.CostEstimate(flops=rows * columns, bytes_accessed=6 * rows * columns, transcendentals=0),
        name="pack_other" if other else "pack_own",
    )(odd, grad)


def places_kernel(places_ref, out_ref):
    replicas, count, spans = places_ref.shape
    half = spans // 2
    source = lax.broadcasted_iota(jnp.int32, (spans, half), 0)
    target = lax.broadcasted_iota(jnp.int32, (spans, half), 1)
    places = places_ref[...].reshape(replicas * count, spans).astype(f32).astype(bf16)
    for parity in range(2):
        chooser = (source == 2 * target + parity).astype(f32).astype(bf16)
        chosen = jnp.dot(places, chooser, preferred_element_type=f32)
        out_ref[:, parity * count : (parity + 1) * count, :] = chosen.reshape(replicas, count, half)


def split_places(positions):
    replicas, count, spans = positions.shape
    return pl.pallas_call(
        places_kernel,
        out_shape=jax.ShapeDtypeStruct((replicas, 2 * count, spans // 2), f32),
        in_specs=[whole],
        out_specs=whole,
        compiler_params=params,
        cost_estimate=pl.CostEstimate(flops=2 * replicas * count * spans * spans, bytes_accessed=8 * replicas * count * spans, transcendentals=0),
        name="split_places",
    )(positions)


def select(coeffs, places):
    level = lax.broadcasted_iota(jnp.int32, (block, coeffs.shape[1]), 0).astype(f32)
    kept = []
    for parity in range(2):
        mine = coeffs[parity * block : (parity + 1) * block]
        for j in range(keep):
            row = parity * keep + j
            kept.append(jnp.sum(jnp.where(places[row : row + 1] == level, mine, 0.0), axis=0, keepdims=True))
    return jnp.concatenate(kept, axis=0)


def spread(kept, places):
    level = lax.broadcasted_iota(jnp.int32, (block, kept.shape[1]), 0).astype(f32)
    dense = []
    for parity in range(2):
        mine = jnp.zeros(level.shape, f32)
        for j in range(keep):
            row = parity * keep + j
            mine = jnp.where(places[row : row + 1] == level, kept[row : row + 1], mine)
        dense.append(mine)
    return jnp.concatenate(dense, axis=0)


def own_kernel(me_ref, places_ref, moment_ref, table_ref, copies_ref, kept_ref):
    _, count, spans = places_ref.shape
    half = spans // 2
    source = lax.broadcasted_iota(jnp.int32, (spans, half), 0)
    target = lax.broadcasted_iota(jnp.int32, (spans, half), 1)
    places = places_ref[me_ref[0]].astype(f32).astype(bf16)
    split = []
    for parity in range(2):
        chooser = (source == 2 * target + parity).astype(f32).astype(bf16)
        split.append(jnp.dot(places, chooser, preferred_element_type=f32))
    own = jnp.concatenate(split, axis=0)
    copies_ref[...] = jnp.broadcast_to(own[None], copies_ref.shape)
    kept_ref[...] = select(forward(decay_rate * moment_ref[...], table_ref), own)


def own_step(me, positions, moment, table, copies):
    replicas, count, spans = positions.shape
    tiles = moment.shape[0]
    return pl.pallas_call(
        own_kernel,
        in_specs=[pl.BlockSpec(memory_space=pltpu.SMEM), whole, whole, whole],
        out_specs=[whole, whole],
        out_shape=[
            jax.ShapeDtypeStruct((copies, 2 * count, spans // 2), f32),
            jax.ShapeDtypeStruct((2 * count, spans // 2), f32),
        ],
        compiler_params=params,
        cost_estimate=pl.CostEstimate(flops=12 * moment.size * lanes, bytes_accessed=8 * moment.size, transcendentals=0),
        name="own_step",
    )(me, positions, moment, table)


def share_kernel(sums_ref, places_ref, table_ref, kept_ref):
    for row in range(sums_ref.shape[0]):
        kept_ref[row] = select(forward(sums_ref[row], table_ref), places_ref[row])


def share_step(sums, places, table):
    return pl.pallas_call(
        share_kernel,
        in_specs=[whole, whole, whole],
        out_specs=whole,
        out_shape=jax.ShapeDtypeStruct(places.shape, f32),
        compiler_params=params,
        cost_estimate=pl.CostEstimate(flops=6 * sums.size * lanes, bytes_accessed=4 * sums.size, transcendentals=0),
        name="share_step",
    )(sums, places, table)


def kept_kernel(shares_ref, kept_ref, copies_ref, out_ref):
    total = kept_ref[...]
    for source in range(shares_ref.shape[0]):
        total = total + shares_ref[source]
    out_ref[...] = total
    copies_ref[...] = jnp.broadcast_to(total[None], copies_ref.shape)


def kept_step(shares, kept, replicas):
    return pl.pallas_call(
        kept_kernel,
        in_specs=[whole, whole],
        out_specs=[whole, whole],
        out_shape=[
            jax.ShapeDtypeStruct((replicas,) + kept.shape, f32),
            jax.ShapeDtypeStruct(kept.shape, f32),
        ],
        compiler_params=params,
        cost_estimate=pl.CostEstimate(flops=shares.size, bytes_accessed=4 * shares.size, transcendentals=0),
        name="kept_step",
    )(shares, kept)


def moment_kernel(parts_ref, moment_ref, kept_ref, places_ref, table_ref, new_ref):
    gradient = parts_ref[0]
    for source in range(1, parts_ref.shape[0]):
        gradient = gradient + parts_ref[source]
    dense = spread(kept_ref[...], places_ref[0])
    new_ref[...] = decay_rate * moment_ref[...] + gradient - inverse(dense, table_ref)


def moment_step(parts, moment, kept, places, table):
    return pl.pallas_call(
        moment_kernel,
        in_specs=[whole] * 5,
        out_specs=whole,
        out_shape=jax.ShapeDtypeStruct(moment.shape, f32),
        compiler_params=params,
        cost_estimate=pl.CostEstimate(flops=6 * moment.size * lanes, bytes_accessed=4 * parts.size, transcendentals=0),
        name="moment_step",
    )(parts, moment, kept, places, table)


def update_kernel(kept_ref, places_ref, table_ref, out_ref):
    replicas, _, half = kept_ref.shape
    sums = []
    for parity in range(2):
        columns = []
        for first in range(0, half, lanes):
            at = slice(first, min(first + lanes, half))
            level = lax.broadcasted_iota(jnp.int32, (block, at.stop - first), 0).astype(f32)

            def one_replica(r, total):
                dense = jnp.zeros(level.shape, f32)
                for j in range(keep):
                    row = pl.ds(parity * keep + j, 1)
                    dense = jnp.where(places_ref[r, row, at] == level, kept_ref[r, row, at], dense)
                return total + dense

            columns.append(lax.fori_loop(0, replicas, one_replica, jnp.zeros(level.shape, f32), unroll=4))
        sums.append(jnp.concatenate(columns, axis=1))
    averaged = inverse(jnp.concatenate(sums, axis=0), table_ref) * (1.0 / replicas)
    squares = averaged * averaged
    high, low = halves(squares)
    row = lax.broadcasted_iota(jnp.int32, (lanes, lanes), 0) // block
    column = lax.broadcasted_iota(jnp.int32, (lanes, lanes), 1) // block
    same = (row == column).astype(f32).astype(bf16)
    meansq = jnp.dot(high, same, preferred_element_type=f32) + jnp.dot(low, same, preferred_element_type=f32)
    out_ref[...] = averaged * lax.rsqrt(squares + meansq * (1.0 / block) + epsilon)


def update_step(kept, places, table):
    replicas, _, half = kept.shape
    return pl.pallas_call(
        update_kernel,
        out_shape=jax.ShapeDtypeStruct((half, lanes), f32),
        in_specs=[whole] * 3,
        out_specs=whole,
        compiler_params=params,
        cost_estimate=pl.CostEstimate(flops=9 * replicas * lanes * half, bytes_accessed=8 * kept.size, transcendentals=lanes * half),
        name="update_step",
    )(kept, places, table)


def body(grad_parts, momentum, positions):
    columns = momentum.shape[-1]
    tiles = columns // lanes
    devices = lax.axis_size("fsdp")
    me = lax.axis_index("fsdp")
    odd = (me % 2).reshape(1)
    grad = grad_parts[0, 0]
    table = jnp.asarray(split_table())
    groups = [list(range(core, devices, 2)) for core in range(2)]

    def along_z(x):
        return lax.all_to_all(x, "fsdp", 0, 0, tiled=True, axis_index_groups=groups)

    moment = momentum.reshape(tiles, lanes)
    positions = positions[:, 0]
    own_places, own_kept = own_step(lax.axis_index("dp").reshape(1), positions, moment, table, devices // 2)
    arrived = lax.ppermute(pack(grad, odd, True), "fsdp", [(i, i ^ 1) for i in range(devices)])
    row_places = along_z(own_places)
    sums = pack(grad, odd, False) + arrived
    gradient = lax.psum_scatter(sums, "fsdp", scatter_dimension=0, tiled=True, axis_index_groups=groups)
    shares = along_z(share_step(sums, row_places, table))
    copies, kept = kept_step(shares, own_kept, positions.shape[0])
    everyone = lax.all_to_all(copies, "dp", 0, 0, tiled=True)
    new_moment = moment_step(gradient.reshape(1, tiles, lanes), moment, kept, own_places, table)
    update = update_step(everyone, split_places(positions), table)
    return update.reshape(1, columns), new_moment.reshape(1, 1, columns)


def solution(mesh):
    in_specs = (P("dp", "fsdp", None, None), P("dp", "fsdp", None), P(None, "fsdp", None, None))
    out_specs = (P("fsdp", None), P("dp", "fsdp", None))
    return jax.shard_map(body, mesh=mesh, in_specs=in_specs, out_specs=out_specs, check_vma=False)
```

```python
import functools

import jax
import jax.numpy as jnp
import numpy as np
from jax import lax
from jax.experimental import pallas as pl
from jax.experimental.pallas import tpu as pltpu
from jax.sharding import PartitionSpec as P

decay_rate = 0.999
epsilon = 1e-06
block = 64
lanes = 128
keep = 4
f32, bf16 = jnp.float32, jnp.bfloat16
whole = pl.BlockSpec(memory_space=pltpu.VMEM)
smem = pl.BlockSpec(memory_space=pltpu.SMEM)
params = pltpu.CompilerParams(vmem_limit_bytes=12 * 2**20)


def paired_table():
    frequency = np.arange(block)[:, None]
    sample = np.arange(block)[None, :]
    cosines = np.cos(np.pi * (2.0 * sample + 1.0) * frequency / (2.0 * block))
    norming = np.where(frequency == 0, np.sqrt(1.0 / block), np.sqrt(2.0 / block))
    return np.kron(np.eye(2), cosines * norming).astype(np.float32)


def tables():
    table = paired_table()
    high = table.astype(jnp.bfloat16)
    low = (table - high.astype(np.float32)).astype(jnp.bfloat16)
    none = np.zeros_like(high)
    ones = np.kron(np.eye(2), np.ones((block, block))).astype(jnp.bfloat16)
    return (
        np.block([[high, high], [low, none]]),
        np.block([[high, low], [high, none]]),
        np.concatenate([ones, ones]),
    )


def halves(x):
    high = x.astype(bf16)
    return high, (x - high.astype(f32)).astype(bf16)


def forward(fields, table_ref):
    parts = jnp.concatenate(halves(fields), axis=1)
    both = lax.dot_general(table_ref[...], parts, (((1,), (1,)), ((), ())), preferred_element_type=f32)
    return both[:lanes] + both[lanes:]


def inverse(coeffs, table_ref):
    parts = jnp.concatenate(halves(coeffs), axis=0)
    both = lax.dot_general(parts, table_ref[...], (((0,), (0,)), ((), ())), preferred_element_type=f32)
    return both[:, :lanes] + both[:, lanes:]


def block_sums(coeffs, ones_ref):
    parts = jnp.concatenate(halves(coeffs), axis=0)
    return lax.dot_general(parts, ones_ref[...], (((0,), (0,)), ((), ())), preferred_element_type=f32)


def same_core_rows(x, odd):
    upper, lower = x[:8], x[8:]
    row = lax.broadcasted_iota(jnp.int32, upper.shape, 0)
    even_place = row % 2 == 0
    return jnp.where(
        odd,
        jnp.where(even_place, pltpu.roll(upper, 7, 0), lower),
        jnp.where(even_place, upper, pltpu.roll(lower, 1, 0)),
    )


def pack_kernel(other, odd_ref, grad_ref, out_ref):
    odd = (odd_ref[0] != 0) != other
    for first in range(0, out_ref.shape[1], 8):
        mixed = jnp.stack(
            [
                same_core_rows(grad_ref[:, tile * lanes : (tile + 1) * lanes], odd)
                for tile in range(first, first + 8)
            ]
        )
        rows = jnp.swapaxes(mixed, 0, 1)
        for place in range(8):
            out_ref[place // 2 + 4 * (place % 2), first : first + 8, :] = rows[place]


def pack(grad, odd, other):
    rows, columns = grad.shape
    return pl.pallas_call(
        functools.partial(pack_kernel, other),
        in_specs=[smem, whole],
        out_specs=whole,
        out_shape=jax.ShapeDtypeStruct((rows // 2, columns // lanes, lanes), f32),
        compiler_params=params,
        cost_estimate=pl.CostEstimate(flops=rows * columns, bytes_accessed=6 * rows * columns, transcendentals=0),
        name="pack_other" if other else "pack_own",
    )(odd, grad)


def places_kernel(places_ref, out_ref):
    replicas, count, spans = places_ref.shape
    half = spans // 2
    source = lax.broadcasted_iota(jnp.int32, (spans, half), 0)
    target = lax.broadcasted_iota(jnp.int32, (spans, half), 1)
    places = places_ref[...].reshape(replicas * count, spans).astype(f32).astype(bf16)
    for parity in range(2):
        chooser = (source == 2 * target + parity).astype(f32).astype(bf16)
        chosen = jnp.dot(places, chooser, preferred_element_type=f32)
        out_ref[:, parity * count : (parity + 1) * count, :] = chosen.reshape(replicas, count, half)


def split_places(positions):
    replicas, count, spans = positions.shape
    return pl.pallas_call(
        places_kernel,
        out_shape=jax.ShapeDtypeStruct((replicas, 2 * count, spans // 2), f32),
        in_specs=[whole],
        out_specs=whole,
        compiler_params=params,
        cost_estimate=pl.CostEstimate(flops=2 * replicas * count * spans * spans, bytes_accessed=8 * replicas * count * spans, transcendentals=0),
        name="split_places",
    )(positions)


def kept_kernel(me_ref, parts_ref, moment_ref, places_ref, table_ref, copies_ref, accumulated_ref):
    gradient = parts_ref[0]
    for source in range(1, parts_ref.shape[0]):
        gradient = gradient + parts_ref[source]
    accumulated = decay_rate * moment_ref[...] + gradient
    accumulated_ref[...] = accumulated
    coeffs = forward(accumulated, table_ref)
    level = lax.broadcasted_iota(jnp.int32, (block, coeffs.shape[1]), 0).astype(f32)
    own = places_ref[me_ref[0]]
    kept = []
    for parity in range(2):
        mine = coeffs[parity * block : (parity + 1) * block]
        for j in range(keep):
            row = parity * keep + j
            kept.append(jnp.sum(jnp.where(own[row : row + 1] == level, mine, 0.0), axis=0, keepdims=True))
    copies_ref[...] = jnp.broadcast_to(jnp.concatenate(kept, axis=0)[None], copies_ref.shape)


def kept_step(me, parts, moment, places, table):
    return pl.pallas_call(
        kept_kernel,
        in_specs=[smem] + [whole] * 4,
        out_specs=[whole, whole],
        out_shape=[
            jax.ShapeDtypeStruct(places.shape, f32),
            jax.ShapeDtypeStruct(moment.shape, f32),
        ],
        compiler_params=params,
        cost_estimate=pl.CostEstimate(flops=6 * moment.size * lanes, bytes_accessed=4 * parts.size, transcendentals=0),
        name="kept_step",
    )(me, parts, moment, places, table)


def dense_of(kept_ref, places_ref, replica, parity, at, level):
    dense = jnp.zeros(level.shape, f32)
    for j in range(keep):
        row = pl.ds(parity * keep + j, 1)
        dense = jnp.where(places_ref[replica, row, at] == level, kept_ref[replica, row, at], dense)
    return dense


def outputs_kernel(me_ref, kept_ref, places_ref, accumulated_ref, table_ref, ones_ref, update_ref, moment_ref):
    replicas, _, half = kept_ref.shape
    for first in range(0, half, lanes):
        at = slice(first, min(first + lanes, half))
        level = lax.broadcasted_iota(jnp.int32, (block, at.stop - first), 0).astype(f32)
        own, sums = [], []
        for parity in range(2):
            own.append(dense_of(kept_ref, places_ref, me_ref[0], parity, at, level))
            total = jnp.zeros(level.shape, f32)
            for replica in range(replicas):
                total = total + dense_of(kept_ref, places_ref, replica, parity, at, level)
            sums.append(total * (1.0 / replicas))
        moment_ref[at, :] = accumulated_ref[at, :] - inverse(jnp.concatenate(own, axis=0), table_ref)
        mean = jnp.concatenate(sums, axis=0)
        averaged = inverse(mean, table_ref)
        meansq = block_sums(mean * mean, ones_ref) * (1.0 / block)
        update_ref[at, :] = averaged * lax.rsqrt(averaged * averaged + meansq + epsilon)


def outputs_step(me, kept, places, accumulated, table, ones):
    replicas, _, half = kept.shape
    return pl.pallas_call(
        outputs_kernel,
        in_specs=[smem] + [whole] * 5,
        out_specs=[whole, whole],
        out_shape=[jax.ShapeDtypeStruct(accumulated.shape, f32)] * 2,
        compiler_params=params,
        cost_estimate=pl.CostEstimate(flops=9 * replicas * lanes * half, bytes_accessed=8 * kept.size, transcendentals=lanes * half),
        name="outputs_step",
    )(me, kept, places, accumulated, table, ones)


def body(grad_parts, momentum, positions):
    columns = momentum.shape[-1]
    tiles = columns // lanes
    devices = lax.axis_size("fsdp")
    me = lax.axis_index("fsdp")
    odd = (me % 2).reshape(1)
    grad = grad_parts[0, 0]
    forward_table, inverse_table, ones = (jnp.asarray(table) for table in tables())
    replica = lax.axis_index("dp").reshape(1)
    sent = pack(grad, odd, True)
    arrived = lax.ppermute(sent, "fsdp", [(i, i ^ 1) for i in range(devices)])
    own = pack(grad, odd, False)
    places = split_places(positions[:, 0])
    own, places, arrived, replica = lax.optimization_barrier((own, places, arrived, replica))
    groups = [list(range(core, devices, 2)) for core in range(2)]
    parts = lax.all_to_all(own + arrived, "fsdp", 0, 0, tiled=True, axis_index_groups=groups)
    copies, accumulated = kept_step(replica, parts, momentum.reshape(tiles, lanes), places, forward_table)
    everyone = lax.all_to_all(copies, "dp", 0, 0, tiled=True)
    update, new_moment = outputs_step(replica, everyone, places, accumulated, inverse_table, ones)
    return update.reshape(1, columns), new_moment.reshape(1, 1, columns)


def solution(mesh):
    in_specs = (P("dp", "fsdp", None, None), P("dp", "fsdp", None), P(None, "fsdp", None, None))
    out_specs = (P("fsdp", None), P("dp", "fsdp", None))
    return jax.shard_map(body, mesh=mesh, in_specs=in_specs, out_specs=out_specs, check_vma=False)
```

```python
import functools

import jax
import jax.numpy as jnp
import numpy as np
from jax import lax
from jax.experimental import pallas as pl
from jax.experimental.pallas import tpu as pltpu
from jax.sharding import PartitionSpec as P

decay_rate = 0.999
epsilon = 1e-06
block = 64
lanes = 128
keep = 4
f32, bf16 = jnp.float32, jnp.bfloat16
whole = pl.BlockSpec(memory_space=pltpu.VMEM)
smem = pl.BlockSpec(memory_space=pltpu.SMEM)
params = pltpu.CompilerParams(vmem_limit_bytes=12 * 2**20)


def paired_table():
    frequency = np.arange(block)[:, None]
    sample = np.arange(block)[None, :]
    cosines = np.cos(np.pi * (2.0 * sample + 1.0) * frequency / (2.0 * block))
    norming = np.where(frequency == 0, np.sqrt(1.0 / block), np.sqrt(2.0 / block))
    return np.kron(np.eye(2), cosines * norming).astype(np.float32)


def tables():
    table = paired_table()
    high = table.astype(jnp.bfloat16)
    low = (table - high.astype(np.float32)).astype(jnp.bfloat16)
    none = np.zeros_like(high)
    ones = np.kron(np.eye(2), np.ones((block, block))).astype(jnp.bfloat16)
    return (
        np.block([[high, high], [low, none]]),
        np.block([[high, low], [high, none]]),
        np.concatenate([ones, ones]),
    )


def halves(x):
    high = x.astype(bf16)
    return high, (x - high.astype(f32)).astype(bf16)


def forward(fields, table_ref):
    parts = jnp.concatenate(halves(fields), axis=1)
    both = lax.dot_general(table_ref[...], parts, (((1,), (1,)), ((), ())), preferred_element_type=f32)
    return both[:lanes] + both[lanes:]


def inverse(coeffs, table_ref):
    parts = jnp.concatenate(halves(coeffs), axis=0)
    both = lax.dot_general(parts, table_ref[...], (((0,), (0,)), ((), ())), preferred_element_type=f32)
    return both[:, :lanes] + both[:, lanes:]


def block_sums(coeffs, ones_ref):
    parts = jnp.concatenate(halves(coeffs), axis=0)
    return lax.dot_general(parts, ones_ref[...], (((0,), (0,)), ((), ())), preferred_element_type=f32)


def pack_kernel(other, core_ref, grad_ref, out_ref, done):
    core = 1 - core_ref[0] if other else core_ref[0]
    places = grad_ref.shape[2] // 2
    copies = [
        pltpu.make_async_copy(
            grad_ref.at[z // places, :, 2 * (z % places) + core, :], out_ref.at[z], done.at[z]
        )
        for z in range(out_ref.shape[0])
    ]
    for copy in copies:
        copy.start()
    for copy in copies:
        copy.wait()


def pack(grad, core, other):
    rows, columns = grad.shape
    tiles = columns // lanes
    grouped = grad.reshape(rows // 8, 8, tiles, lanes).transpose(0, 2, 1, 3)
    return pl.pallas_call(
        functools.partial(pack_kernel, other),
        in_specs=[smem, pl.BlockSpec(memory_space=pl.ANY)],
        out_specs=whole,
        out_shape=jax.ShapeDtypeStruct((rows // 2, tiles, lanes), f32),
        scratch_shapes=[pltpu.SemaphoreType.DMA((rows // 2,))],
        compiler_params=pltpu.CompilerParams(vmem_limit_bytes=52 * 2**20),
        cost_estimate=pl.CostEstimate(flops=0, bytes_accessed=4 * rows * columns, transcendentals=0),
        name="pack_other" if other else "pack_own",
    )(core, grouped)


def places_kernel(places_ref, out_ref):
    replicas, count, spans = places_ref.shape
    half = spans // 2
    source = lax.broadcasted_iota(jnp.int32, (spans, half), 0)
    target = lax.broadcasted_iota(jnp.int32, (spans, half), 1)
    places = places_ref[...].reshape(replicas * count, spans).astype(f32).astype(bf16)
    for parity in range(2):
        chooser = (source == 2 * target + parity).astype(f32).astype(bf16)
        chosen = jnp.dot(places, chooser, preferred_element_type=f32)
        out_ref[:, parity * count : (parity + 1) * count, :] = chosen.reshape(replicas, count, half)


def split_places(positions):
    replicas, count, spans = positions.shape
    return pl.pallas_call(
        places_kernel,
        out_shape=jax.ShapeDtypeStruct((replicas, 2 * count, spans // 2), f32),
        in_specs=[whole],
        out_specs=whole,
        compiler_params=params,
        cost_estimate=pl.CostEstimate(flops=2 * replicas * count * spans * spans, bytes_accessed=8 * replicas * count * spans, transcendentals=0),
        name="split_places",
    )(positions)


def kept_kernel(me_ref, parts_ref, moment_ref, places_ref, table_ref, copies_ref, accumulated_ref):
    gradient = parts_ref[0]
    for source in range(1, parts_ref.shape[0]):
        gradient = gradient + parts_ref[source]
    accumulated = decay_rate * moment_ref[...] + gradient
    accumulated_ref[...] = accumulated
    coeffs = forward(accumulated, table_ref)
    level = lax.broadcasted_iota(jnp.int32, (block, coeffs.shape[1]), 0).astype(f32)
    own = places_ref[me_ref[0]]
    kept = []
    for parity in range(2):
        mine = coeffs[parity * block : (parity + 1) * block]
        for j in range(keep):
            row = parity * keep + j
            kept.append(jnp.sum(jnp.where(own[row : row + 1] == level, mine, 0.0), axis=0, keepdims=True))
    copies_ref[...] = jnp.broadcast_to(jnp.concatenate(kept, axis=0)[None], copies_ref.shape)


def kept_step(me, parts, moment, places, table):
    return pl.pallas_call(
        kept_kernel,
        in_specs=[smem] + [whole] * 4,
        out_specs=[whole, whole],
        out_shape=[
            jax.ShapeDtypeStruct(places.shape, f32),
            jax.ShapeDtypeStruct(moment.shape, f32),
        ],
        compiler_params=params,
        cost_estimate=pl.CostEstimate(flops=6 * moment.size * lanes, bytes_accessed=4 * parts.size, transcendentals=0),
        name="kept_step",
    )(me, parts, moment, places, table)


def dense_of(kept_ref, places_ref, replica, parity, at, level):
    dense = jnp.zeros(level.shape, f32)
    for j in range(keep):
        row = pl.ds(parity * keep + j, 1)
        dense = jnp.where(places_ref[replica, row, at] == level, kept_ref[replica, row, at], dense)
    return dense


def outputs_kernel(me_ref, kept_ref, places_ref, accumulated_ref, table_ref, ones_ref, update_ref, moment_ref, update, moment, done):
    replicas, _, half = kept_ref.shape
    copies = []

    def send(source, target, at):
        copies.append(pltpu.make_async_copy(source.at[at], target.at[at], done.at[len(copies)]))
        copies[-1].start()

    own = []
    level = lax.broadcasted_iota(jnp.int32, (block, half), 0).astype(f32)
    for parity in range(2):
        own.append(dense_of(kept_ref, places_ref, me_ref[0], parity, slice(0, half), level))
    moment[...] = accumulated_ref[...] - inverse(jnp.concatenate(own, axis=0), table_ref)
    send(moment, moment_ref, slice(0, half))
    for first in range(0, half, lanes):
        at = slice(first, min(first + lanes, half))
        level = lax.broadcasted_iota(jnp.int32, (block, at.stop - first), 0).astype(f32)
        sums = []
        for parity in range(2):
            total = jnp.zeros(level.shape, f32)
            for replica in range(replicas):
                total = total + dense_of(kept_ref, places_ref, replica, parity, at, level)
            sums.append(total * (1.0 / replicas))
        mean = jnp.concatenate(sums, axis=0)
        averaged = inverse(mean, table_ref)
        meansq = block_sums(mean * mean, ones_ref) * (1.0 / block)
        update[at, :] = averaged * lax.rsqrt(averaged * averaged + meansq + epsilon)
        send(update, update_ref, at)
    for copy in copies:
        copy.wait()


def outputs_step(me, kept, places, accumulated, table, ones):
    replicas, _, half = kept.shape
    return pl.pallas_call(
        outputs_kernel,
        in_specs=[smem] + [whole] * 5,
        out_specs=[pl.BlockSpec(memory_space=pl.ANY)] * 2,
        out_shape=[jax.ShapeDtypeStruct(accumulated.shape, f32)] * 2,
        scratch_shapes=[
            pltpu.VMEM(accumulated.shape, f32),
            pltpu.VMEM(accumulated.shape, f32),
            pltpu.SemaphoreType.DMA((1 + pl.cdiv(half, lanes),)),
        ],
        compiler_params=params,
        cost_estimate=pl.CostEstimate(flops=9 * replicas * lanes * half, bytes_accessed=8 * kept.size, transcendentals=lanes * half),
        name="outputs_step",
    )(me, kept, places, accumulated, table, ones)


def body(grad_parts, momentum, positions):
    columns = momentum.shape[-1]
    tiles = columns // lanes
    devices = lax.axis_size("fsdp")
    me = lax.axis_index("fsdp")
    core = (me % 2).reshape(1)
    grad = grad_parts[0, 0]
    forward_table, inverse_table, ones = (jnp.asarray(table) for table in tables())
    replica = lax.axis_index("dp").reshape(1)
    sent = pack(grad, core, True)
    arrived = lax.ppermute(sent, "fsdp", [(i, i ^ 1) for i in range(devices)])
    own = pack(grad, core, False)
    places = split_places(positions[:, 0])
    own, places, arrived, replica = lax.optimization_barrier((own, places, arrived, replica))
    groups = [list(range(core, devices, 2)) for core in range(2)]
    parts = lax.all_to_all(own + arrived, "fsdp", 0, 0, tiled=True, axis_index_groups=groups)
    copies, accumulated = kept_step(replica, parts, momentum.reshape(tiles, lanes), places, forward_table)
    everyone = lax.all_to_all(copies, "dp", 0, 0, tiled=True)
    update, new_moment = outputs_step(replica, everyone, places, accumulated, inverse_table, ones)
    return update.reshape(1, columns), new_moment.reshape(1, 1, columns)


def solution(mesh):
    in_specs = (P("dp", "fsdp", None, None), P("dp", "fsdp", None), P(None, "fsdp", None, None))
    out_specs = (P("fsdp", None), P("dp", "fsdp", None))
    return jax.shard_map(body, mesh=mesh, in_specs=in_specs, out_specs=out_specs, check_vma=False)
```

```python
import functools

import jax
import jax.numpy as jnp
import numpy as np
from jax import lax
from jax.experimental import pallas as pl
from jax.experimental.pallas import tpu as pltpu
from jax.sharding import PartitionSpec as P

decay_rate = 0.999
epsilon = 1e-06
block = 64
lanes = 128
keep = 4
f32, bf16 = jnp.float32, jnp.bfloat16
whole = pl.BlockSpec(memory_space=pltpu.VMEM)
smem = pl.BlockSpec(memory_space=pltpu.SMEM)
anywhere = pl.BlockSpec(memory_space=pl.ANY)
params = pltpu.CompilerParams(vmem_limit_bytes=12 * 2**20)
narrow = pltpu.CompilerParams(vmem_limit_bytes=51 * 2**20)


def paired_table():
    frequency = np.arange(block)[:, None]
    sample = np.arange(block)[None, :]
    cosines = np.cos(np.pi * (2.0 * sample + 1.0) * frequency / (2.0 * block))
    norming = np.where(frequency == 0, np.sqrt(1.0 / block), np.sqrt(2.0 / block))
    return np.kron(np.eye(2), cosines * norming).astype(np.float32)


def tables():
    table = paired_table()
    high = table.astype(jnp.bfloat16)
    low = (table - high.astype(np.float32)).astype(jnp.bfloat16)
    none = np.zeros_like(high)
    return np.block([[high, high], [low, none]]), np.block([[high.T, high.T], [low.T, none]])


def halves(x):
    high = x.astype(bf16)
    return high, (x - high.astype(f32)).astype(bf16)


def forward(fields, table_ref):
    parts = jnp.concatenate(halves(fields), axis=1)
    both = lax.dot_general(table_ref[...], parts, (((1,), (1,)), ((), ())), preferred_element_type=f32)
    return both[:lanes] + both[lanes:]


def inverse(coeffs, table_ref):
    parts = jnp.concatenate(halves(coeffs), axis=0)
    both = jnp.dot(table_ref[...], parts, preferred_element_type=f32)
    return both[:lanes] + both[lanes:]


def row_copies(core, grad_ref, out_ref, done):
    places = grad_ref.shape[2] // 2
    return [
        pltpu.make_async_copy(
            grad_ref.at[z // places, :, 2 * (z % places) + core, :], out_ref.at[z], done.at[z]
        )
        for z in range(out_ref.shape[0])
    ]


def pack_kernel(core_ref, grad_ref, out_ref, done):
    copies = row_copies(1 - core_ref[0], grad_ref, out_ref, done)
    for copy in copies:
        copy.start()
    for copy in copies:
        copy.wait()


def pack_other(grouped, core):
    groups, tiles, places, _ = grouped.shape
    rows = groups * places // 2
    return pl.pallas_call(
        pack_kernel,
        in_specs=[smem, anywhere],
        out_specs=whole,
        out_shape=jax.ShapeDtypeStruct((rows, tiles, lanes), f32),
        scratch_shapes=[pltpu.SemaphoreType.DMA((rows,))],
        compiler_params=pltpu.CompilerParams(vmem_limit_bytes=52 * 2**20),
        cost_estimate=pl.CostEstimate(flops=0, bytes_accessed=4 * grouped.size, transcendentals=0),
        name="pack_other",
    )(core, grouped)


def prepare_kernel(core_ref, me_ref, grad_ref, places_ref, own_ref, index_ref, mine_ref, split, done):
    copies = row_copies(core_ref[0], grad_ref, own_ref, done)
    for copy in copies:
        copy.start()
    replicas, count, spans = places_ref.shape
    half = spans // 2
    source = lax.broadcasted_iota(jnp.int32, (spans, half), 0)
    target = lax.broadcasted_iota(jnp.int32, (spans, half), 1)
    places = places_ref[...].reshape(replicas * count, spans).astype(f32).astype(bf16)
    for parity in range(2):
        chooser = (source == 2 * target + parity).astype(f32).astype(bf16)
        chosen = jnp.dot(places, chooser, preferred_element_type=f32)
        split[:, parity * count : (parity + 1) * count, :] = chosen.reshape(replicas, count, half)
    mine_ref[...] = split[me_ref[0]]
    level = lax.broadcasted_iota(jnp.int32, (block, half), 0).astype(f32)
    for parity in range(2):
        nothing = count * (1 - parity)
        for word in range(replicas // 8):
            packed = jnp.zeros(level.shape, jnp.int32)
            for field in range(8):
                row_of = jnp.full(level.shape, nothing << (4 * field), jnp.int32)
                for j in range(count):
                    row = parity * count + j
                    here = split[word * 8 + field, row : row + 1, :] == level
                    row_of = jnp.where(here, row << (4 * field), row_of)
                packed = packed | row_of
            index_ref[word, parity * block : (parity + 1) * block, :] = packed
    for copy in copies:
        copy.wait()


def prepare(core, me, grouped, positions):
    groups, tiles, places, _ = grouped.shape
    rows = groups * places // 2
    replicas, count, spans = positions.shape
    half = spans // 2
    return pl.pallas_call(
        prepare_kernel,
        in_specs=[smem, smem, anywhere, whole],
        out_specs=[whole] * 3,
        out_shape=[
            jax.ShapeDtypeStruct((rows, tiles, lanes), f32),
            jax.ShapeDtypeStruct((replicas // 8, 2 * block, half), jnp.int32),
            jax.ShapeDtypeStruct((2 * count, half), f32),
        ],
        scratch_shapes=[
            pltpu.VMEM((replicas, 2 * count, half), f32),
            pltpu.SemaphoreType.DMA((rows,)),
        ],
        compiler_params=narrow,
        cost_estimate=pl.CostEstimate(flops=9 * replicas * lanes * half, bytes_accessed=4 * grouped.size, transcendentals=0),
        name="prepare",
    )(core, me, grouped, positions)


def kept_kernel(parts_ref, moment_ref, places_ref, table_ref, copies_ref, accumulated_ref):
    gradient = parts_ref[0]
    for source in range(1, parts_ref.shape[0]):
        gradient = gradient + parts_ref[source]
    accumulated = decay_rate * moment_ref[...] + gradient
    accumulated_ref[...] = accumulated
    coeffs = forward(accumulated, table_ref)
    level = lax.broadcasted_iota(jnp.int32, (block, coeffs.shape[1]), 0).astype(f32)
    own = places_ref[...]
    kept = []
    for parity in range(2):
        mine = coeffs[parity * block : (parity + 1) * block]
        for j in range(keep):
            row = parity * keep + j
            kept.append(jnp.sum(jnp.where(own[row : row + 1] == level, mine, 0.0), axis=0, keepdims=True))
    copies_ref[...] = jnp.broadcast_to(jnp.concatenate(kept, axis=0)[None], copies_ref.shape)


def kept_step(parts, moment, places, table, replicas):
    return pl.pallas_call(
        kept_kernel,
        in_specs=[whole] * 4,
        out_specs=[whole, whole],
        out_shape=[
            jax.ShapeDtypeStruct((replicas,) + places.shape, f32),
            jax.ShapeDtypeStruct(moment.shape, f32),
        ],
        compiler_params=params,
        cost_estimate=pl.CostEstimate(flops=6 * moment.size * lanes, bytes_accessed=4 * parts.size, transcendentals=0),
        name="kept_step",
    )(parts, moment, places, table)


def by_parity(values):
    even = lax.broadcasted_iota(jnp.int32, values.shape, 0) < keep
    return jnp.where(even, values, 0.0), jnp.where(even, 0.0, values)


def placed(values, word, shift):
    rows = lax.shift_right_logical(word, jnp.full(word.shape, shift, jnp.int32)) & 7
    return jnp.take_along_axis(values, rows, axis=0, mode="promise_in_bounds")


def outputs_kernel(me_ref, kept_ref, index_ref, accumulated_ref, table_ref, update_ref, moment_ref, update, moment, done):
    replicas, _, half = kept_ref.shape
    chunks = range(0, 2 * block, 8)
    copies = []

    def send(source, target, at):
        copies.append(pltpu.make_async_copy(source.at[at], target.at[at], done.at[len(copies)]))
        copies[-1].start()

    me = me_ref[0]
    sides = by_parity(kept_ref[me])
    own = [placed(sides[k // block], index_ref[me // 8, k : k + 8, :], me % 8 * 4) for k in chunks]
    moment[...] = accumulated_ref[...] - inverse(jnp.concatenate(own, axis=0), table_ref).T
    send(moment, moment_ref, slice(0, half))
    for first in range(0, half, lanes):
        at = slice(first, min(first + lanes, half))
        sums = [jnp.zeros((8, at.stop - first), f32) for _ in chunks]
        for replica in range(replicas):
            sides = by_parity(kept_ref[replica, :, at])
            sums = [
                total + placed(sides[k // block], index_ref[replica // 8, k : k + 8, at], replica % 8 * 4)
                for k, total in zip(chunks, sums)
            ]
        mean = jnp.concatenate(sums, axis=0) * (1.0 / replicas)
        averaged = inverse(mean, table_ref)
        parts = []
        for side in (slice(0, block), slice(block, 2 * block)):
            meansq = jnp.sum(mean[side] * mean[side], axis=0, keepdims=True) * (1.0 / block)
            parts.append(averaged[side] * lax.rsqrt(averaged[side] * averaged[side] + (meansq + epsilon)))
        update[at, :] = jnp.concatenate(parts, axis=0).T
        send(update, update_ref, at)
    for copy in copies:
        copy.wait()


def outputs_step(me, kept, index, accumulated, table):
    replicas, _, half = kept.shape
    return pl.pallas_call(
        outputs_kernel,
        in_specs=[smem] + [whole] * 4,
        out_specs=[anywhere] * 2,
        out_shape=[jax.ShapeDtypeStruct(accumulated.shape, f32)] * 2,
        scratch_shapes=[
            pltpu.VMEM(accumulated.shape, f32),
            pltpu.VMEM(accumulated.shape, f32),
            pltpu.SemaphoreType.DMA((1 + pl.cdiv(half, lanes),)),
        ],
        compiler_params=params,
        cost_estimate=pl.CostEstimate(flops=9 * replicas * lanes * half, bytes_accessed=8 * kept.size, transcendentals=lanes * half),
        name="outputs_step",
    )(me, kept, index, accumulated, table)


def body(grad_parts, momentum, positions):
    columns = momentum.shape[-1]
    tiles = columns // lanes
    devices = lax.axis_size("fsdp")
    me = lax.axis_index("fsdp")
    core = (me % 2).reshape(1)
    rows = grad_parts.shape[2]
    grouped = grad_parts[0, 0].reshape(rows // 8, 8, tiles, lanes).transpose(0, 2, 1, 3)
    positions = positions[:, 0]
    forward_table, inverse_table = (jnp.asarray(table) for table in tables())
    replica = lax.axis_index("dp").reshape(1)
    arrived = lax.ppermute(pack_other(grouped, core), "fsdp", [(i, i ^ 1) for i in range(devices)])
    own, index, places = prepare(core, replica, grouped, positions)
    own, index, places, arrived, replica = lax.optimization_barrier((own, index, places, arrived, replica))
    groups = [list(range(side, devices, 2)) for side in range(2)]
    parts = lax.all_to_all(own + arrived, "fsdp", 0, 0, tiled=True, axis_index_groups=groups)
    copies, accumulated = kept_step(parts, momentum.reshape(tiles, lanes), places, forward_table, positions.shape[0])
    everyone = lax.all_to_all(copies, "dp", 0, 0, tiled=True)
    update, new_moment = outputs_step(replica, everyone, index, accumulated, inverse_table)
    return update.reshape(1, columns), new_moment.reshape(1, 1, columns)


def solution(mesh):
    in_specs = (P("dp", "fsdp", None, None), P("dp", "fsdp", None), P(None, "fsdp", None, None))
    out_specs = (P("fsdp", None), P("dp", "fsdp", None))
    return jax.shard_map(body, mesh=mesh, in_specs=in_specs, out_specs=out_specs, check_vma=False)
```

```python
import functools

import jax
import jax.numpy as jnp
import numpy as np
from jax import lax
from jax.experimental import pallas as pl
from jax.experimental.pallas import tpu as pltpu
from jax.sharding import PartitionSpec as P

decay_rate = 0.999
epsilon = 1e-06
block = 64
lanes = 128
keep = 4
f32, bf16 = jnp.float32, jnp.bfloat16
whole = pl.BlockSpec(memory_space=pltpu.VMEM)
smem = pl.BlockSpec(memory_space=pltpu.SMEM)
anywhere = pl.BlockSpec(memory_space=pl.ANY)
params = pltpu.CompilerParams(vmem_limit_bytes=12 * 2**20)
narrow = pltpu.CompilerParams(vmem_limit_bytes=51 * 2**20)


def z_order(count):
    return list(range(count - 1, -1, -1))


def dp_order():
    lag_x, lag_y = (0, 6, 9, 13), (0, 4, 12, 18, 31, 26, 24, 23)
    lag = [x + y for x in lag_x for y in lag_y]
    return sorted(range(len(lag)), key=lambda replica: (lag[replica], replica), reverse=True)


def paired_table():
    frequency = np.arange(block)[:, None]
    sample = np.arange(block)[None, :]
    cosines = np.cos(np.pi * (2.0 * sample + 1.0) * frequency / (2.0 * block))
    norming = np.where(frequency == 0, np.sqrt(1.0 / block), np.sqrt(2.0 / block))
    return np.kron(np.eye(2), cosines * norming).astype(np.float32)


def tables():
    table = paired_table()
    high = table.astype(jnp.bfloat16)
    low = (table - high.astype(np.float32)).astype(jnp.bfloat16)
    none = np.zeros_like(high)
    return np.block([[high, high], [low, none]]), np.block([[high.T, high.T], [low.T, none]])


def halves(x):
    high = x.astype(bf16)
    return high, (x - high.astype(f32)).astype(bf16)


def forward(fields, table_ref):
    parts = jnp.concatenate(halves(fields), axis=1)
    both = lax.dot_general(table_ref[...], parts, (((1,), (1,)), ((), ())), preferred_element_type=f32)
    return both[:lanes] + both[lanes:]


def inverse(coeffs, table_ref):
    parts = jnp.concatenate(halves(coeffs), axis=0)
    both = jnp.dot(table_ref[...], parts, preferred_element_type=f32)
    return both[:lanes] + both[lanes:]


def row_copies(core, grad_ref, out_ref, done):
    places = grad_ref.shape[2] // 2
    return [
        pltpu.make_async_copy(
            grad_ref.at[z // places, :, 2 * (z % places) + core, :], out_ref.at[z], done.at[z]
        )
        for z in range(out_ref.shape[0])
    ]


def pack_kernel(core_ref, grad_ref, out_ref, done):
    copies = row_copies(1 - core_ref[0], grad_ref, out_ref, done)
    for copy in copies:
        copy.start()
    for copy in copies:
        copy.wait()


def pack_other(grouped, core):
    groups, tiles, places, _ = grouped.shape
    rows = groups * places // 2
    return pl.pallas_call(
        pack_kernel,
        in_specs=[smem, anywhere],
        out_specs=whole,
        out_shape=jax.ShapeDtypeStruct((rows, tiles, lanes), f32),
        scratch_shapes=[pltpu.SemaphoreType.DMA((rows,))],
        compiler_params=pltpu.CompilerParams(vmem_limit_bytes=52 * 2**20),
        cost_estimate=pl.CostEstimate(flops=0, bytes_accessed=4 * grouped.size, transcendentals=0),
        name="pack_other",
    )(core, grouped)


def prepare_kernel(core_ref, me_ref, grad_ref, places_ref, own_ref, index_ref, mine_ref, rows_ref, split, done):
    copies = row_copies(core_ref[0], grad_ref, own_ref, done)
    for copy in copies:
        copy.start()
    replicas, count, spans = places_ref.shape
    half = spans // 2
    source = lax.broadcasted_iota(jnp.int32, (spans, half), 0)
    target = lax.broadcasted_iota(jnp.int32, (spans, half), 1)
    places = places_ref[...].reshape(replicas * count, spans).astype(f32).astype(bf16)
    for parity in range(2):
        chooser = (source == 2 * target + parity).astype(f32).astype(bf16)
        chosen = jnp.dot(places, chooser, preferred_element_type=f32)
        split[:, parity * count : (parity + 1) * count, :] = chosen.reshape(replicas, count, half)
    mine_ref[...] = split[me_ref[0]]
    level = lax.broadcasted_iota(jnp.int32, (block, half), 0).astype(f32)
    order = dp_order()

    def row_of(places, parity, shift):
        rows = jnp.full(level.shape, (count * (1 - parity)) << shift, jnp.int32)
        for j in range(count):
            row = parity * count + j
            rows = jnp.where(places(row) == level, row << shift, rows)
        return rows

    for parity in range(2):
        at = slice(parity * block, (parity + 1) * block)
        rows_ref[at, :] = row_of(lambda row: mine_ref[row : row + 1, :], parity, 0)
        for word in range(replicas // 8):
            packed = jnp.zeros(level.shape, jnp.int32)
            for field in range(8):
                replica = order[word * 8 + field]
                packed = packed | row_of(lambda row: split[replica, row : row + 1, :], parity, 4 * field)
            index_ref[word, at, :] = packed
    for copy in copies:
        copy.wait()


def prepare(core, me, grouped, positions):
    groups, tiles, places, _ = grouped.shape
    rows = groups * places // 2
    replicas, count, spans = positions.shape
    half = spans // 2
    return pl.pallas_call(
        prepare_kernel,
        in_specs=[smem, smem, anywhere, whole],
        out_specs=[whole] * 4,
        out_shape=[
            jax.ShapeDtypeStruct((rows, tiles, lanes), f32),
            jax.ShapeDtypeStruct((replicas // 8, 2 * block, half), jnp.int32),
            jax.ShapeDtypeStruct((2 * count, half), f32),
            jax.ShapeDtypeStruct((2 * block, half), jnp.int32),
        ],
        scratch_shapes=[
            pltpu.VMEM((replicas, 2 * count, half), f32),
            pltpu.SemaphoreType.DMA((rows,)),
        ],
        compiler_params=narrow,
        cost_estimate=pl.CostEstimate(flops=9 * replicas * lanes * half, bytes_accessed=4 * grouped.size, transcendentals=0),
        name="prepare",
    )(core, me, grouped, positions)


def add_kernel(own_ref, arrived_ref, out_ref):
    for place, z in enumerate(z_order(out_ref.shape[0])):
        out_ref[place] = own_ref[z] + arrived_ref[z]


def add_step(own, arrived):
    return pl.pallas_call(
        add_kernel,
        in_specs=[whole, whole],
        out_specs=whole,
        out_shape=jax.ShapeDtypeStruct(own.shape, f32),
        compiler_params=params,
        cost_estimate=pl.CostEstimate(flops=own.size, bytes_accessed=12 * own.size, transcendentals=0),
        name="add_step",
    )(own, arrived)


def kept_kernel(parts_ref, moment_ref, places_ref, table_ref, copies_ref, own_ref, accumulated_ref):
    gradient = parts_ref[0]
    for source in range(1, parts_ref.shape[0]):
        gradient = gradient + parts_ref[source]
    accumulated = decay_rate * moment_ref[...] + gradient
    accumulated_ref[...] = accumulated
    coeffs = forward(accumulated, table_ref)
    level = lax.broadcasted_iota(jnp.int32, (block, coeffs.shape[1]), 0).astype(f32)
    own = places_ref[...]
    kept = []
    for parity in range(2):
        mine = coeffs[parity * block : (parity + 1) * block]
        for j in range(keep):
            row = parity * keep + j
            kept.append(jnp.sum(jnp.where(own[row : row + 1] == level, mine, 0.0), axis=0, keepdims=True))
    own_ref[...] = jnp.concatenate(kept, axis=0)
    copies_ref[...] = jnp.broadcast_to(own_ref[...][None], copies_ref.shape)


def kept_step(parts, moment, places, table, replicas):
    return pl.pallas_call(
        kept_kernel,
        in_specs=[whole] * 4,
        out_specs=[whole] * 3,
        out_shape=[
            jax.ShapeDtypeStruct((replicas,) + places.shape, f32),
            jax.ShapeDtypeStruct(places.shape, f32),
            jax.ShapeDtypeStruct(moment.shape, f32),
        ],
        compiler_params=params,
        cost_estimate=pl.CostEstimate(flops=6 * moment.size * lanes, bytes_accessed=4 * parts.size, transcendentals=0),
        name="kept_step",
    )(parts, moment, places, table)


def by_parity(values):
    even = lax.broadcasted_iota(jnp.int32, values.shape, 0) < keep
    return jnp.where(even, values, 0.0), jnp.where(even, 0.0, values)


def taken(values, rows):
    return jnp.take_along_axis(values, rows, axis=0, mode="promise_in_bounds")


def placed(values, word, shift):
    rows = lax.shift_right_logical(word, jnp.full(word.shape, shift, jnp.int32)) & 7
    return taken(values, rows)


def outputs_kernel(kept_ref, index_ref, own_ref, rows_ref, accumulated_ref, table_ref, update_ref, moment_ref, update, moment, done):
    replicas, _, half = kept_ref.shape
    chunks = range(0, 2 * block, 8)
    copies = []

    def send(source, target, at):
        copies.append(pltpu.make_async_copy(source.at[at], target.at[at], done.at[len(copies)]))
        copies[-1].start()

    sides = by_parity(own_ref[...])
    own = [taken(sides[k // block], rows_ref[k : k + 8, :]) for k in chunks]
    moment[...] = accumulated_ref[...] - inverse(jnp.concatenate(own, axis=0), table_ref).T
    send(moment, moment_ref, slice(0, half))
    for first in range(0, half, lanes):
        at = slice(first, min(first + lanes, half))
        sums = [jnp.zeros((8, at.stop - first), f32) for _ in chunks]
        for replica in range(replicas):
            sides = by_parity(kept_ref[replica, :, at])
            sums = [
                total + placed(sides[k // block], index_ref[replica // 8, k : k + 8, at], replica % 8 * 4)
                for k, total in zip(chunks, sums)
            ]
        mean = jnp.concatenate(sums, axis=0) * (1.0 / replicas)
        averaged = inverse(mean, table_ref)
        parts = []
        for side in (slice(0, block), slice(block, 2 * block)):
            meansq = jnp.sum(mean[side] * mean[side], axis=0, keepdims=True) * (1.0 / block)
            parts.append(averaged[side] * lax.rsqrt(averaged[side] * averaged[side] + (meansq + epsilon)))
        update[at, :] = jnp.concatenate(parts, axis=0).T
        send(update, update_ref, at)
    for copy in copies:
        copy.wait()


def outputs_step(kept, index, own, rows, accumulated, table):
    replicas, _, half = kept.shape
    return pl.pallas_call(
        outputs_kernel,
        in_specs=[whole] * 6,
        out_specs=[anywhere] * 2,
        out_shape=[jax.ShapeDtypeStruct(accumulated.shape, f32)] * 2,
        scratch_shapes=[
            pltpu.VMEM(accumulated.shape, f32),
            pltpu.VMEM(accumulated.shape, f32),
            pltpu.SemaphoreType.DMA((1 + pl.cdiv(half, lanes),)),
        ],
        compiler_params=params,
        cost_estimate=pl.CostEstimate(flops=9 * replicas * lanes * half, bytes_accessed=8 * kept.size, transcendentals=lanes * half),
        name="outputs_step",
    )(kept, index, own, rows, accumulated, table)


def body(grad_parts, momentum, positions):
    columns = momentum.shape[-1]
    tiles = columns // lanes
    devices = lax.axis_size("fsdp")
    me = lax.axis_index("fsdp")
    core = (me % 2).reshape(1)
    rows = grad_parts.shape[2]
    grouped = grad_parts[0, 0].reshape(rows // 8, 8, tiles, lanes).transpose(0, 2, 1, 3)
    positions = positions[:, 0]
    forward_table, inverse_table = (jnp.asarray(table) for table in tables())
    replica = lax.axis_index("dp").reshape(1)
    arrived = lax.ppermute(pack_other(grouped, core), "fsdp", [(i, i ^ 1) for i in range(devices)])
    own, index, places, rows = prepare(core, replica, grouped, positions)
    own, index, places, rows, arrived = lax.optimization_barrier((own, index, places, rows, arrived))
    groups = [[2 * z + side for z in z_order(devices // 2)] for side in range(2)]
    parts = lax.all_to_all(add_step(own, arrived), "fsdp", 0, 0, tiled=True, axis_index_groups=groups)
    copies, kept, accumulated = kept_step(parts, momentum.reshape(tiles, lanes), places, forward_table, positions.shape[0])
    everyone = lax.all_to_all(copies, "dp", 0, 0, tiled=True, axis_index_groups=[dp_order()])
    update, new_moment = outputs_step(everyone, index, kept, rows, accumulated, inverse_table)
    return update.reshape(1, columns), new_moment.reshape(1, 1, columns)


def solution(mesh):
    in_specs = (P("dp", "fsdp", None, None), P("dp", "fsdp", None), P(None, "fsdp", None, None))
    out_specs = (P("fsdp", None), P("dp", "fsdp", None))
    return jax.shard_map(body, mesh=mesh, in_specs=in_specs, out_specs=out_specs, check_vma=False)
```

```python
import functools

import jax
import jax.numpy as jnp
import numpy as np
from jax import lax
from jax.experimental import pallas as pl
from jax.experimental.pallas import tpu as pltpu
from jax.sharding import PartitionSpec as P

decay_rate = 0.999
epsilon = 1e-06
block = 64
lanes = 128
keep = 4
f32, bf16 = jnp.float32, jnp.bfloat16
whole = pl.BlockSpec(memory_space=pltpu.VMEM)
smem = pl.BlockSpec(memory_space=pltpu.SMEM)
anywhere = pl.BlockSpec(memory_space=pl.ANY)
params = pltpu.CompilerParams(vmem_limit_bytes=12 * 2**20)
narrow = pltpu.CompilerParams(vmem_limit_bytes=51 * 2**20)


def z_order(count):
    half = count // 2
    return [z for pair in range(half - 1, -1, -1) for z in (pair + half, pair)]


def dp_order():
    lag_x, lag_y = (0, 6, 9, 13), (0, 4, 12, 18, 31, 26, 24, 23)
    lag = [x + y for x in lag_x for y in lag_y]
    return sorted(range(len(lag)), key=lambda replica: (lag[replica], replica), reverse=True)


def paired_table():
    frequency = np.arange(block)[:, None]
    sample = np.arange(block)[None, :]
    cosines = np.cos(np.pi * (2.0 * sample + 1.0) * frequency / (2.0 * block))
    norming = np.where(frequency == 0, np.sqrt(1.0 / block), np.sqrt(2.0 / block))
    return np.kron(np.eye(2), cosines * norming).astype(np.float32)


def tables():
    table = paired_table()
    high = table.astype(jnp.bfloat16)
    low = (table - high.astype(np.float32)).astype(jnp.bfloat16)
    none = np.zeros_like(high)
    return np.block([[high, high], [low, none]]), np.block([[high.T, high.T], [low.T, none]])


def halves(x):
    high = x.astype(bf16)
    return high, (x - high.astype(f32)).astype(bf16)


def forward(fields, table_ref):
    parts = jnp.concatenate(halves(fields), axis=1)
    both = lax.dot_general(table_ref[...], parts, (((1,), (1,)), ((), ())), preferred_element_type=f32)
    return both[:lanes] + both[lanes:]


def inverse(coeffs, table_ref):
    parts = jnp.concatenate(halves(coeffs), axis=0)
    both = jnp.dot(table_ref[...], parts, preferred_element_type=f32)
    return both[:lanes] + both[lanes:]


def row_copies(core, grad_ref, out_ref, done):
    places = grad_ref.shape[2] // 2
    return [
        pltpu.make_async_copy(
            grad_ref.at[z // places, :, 2 * (z % places) + core, :], out_ref.at[z], done.at[z]
        )
        for z in range(out_ref.shape[0])
    ]


def pack_kernel(core_ref, grad_ref, out_ref, done):
    copies = row_copies(1 - core_ref[0], grad_ref, out_ref, done)
    for copy in copies:
        copy.start()
    for copy in copies:
        copy.wait()


def pack_other(grouped, core):
    groups, tiles, places, _ = grouped.shape
    rows = groups * places // 2
    return pl.pallas_call(
        pack_kernel,
        in_specs=[smem, anywhere],
        out_specs=whole,
        out_shape=jax.ShapeDtypeStruct((rows, tiles, lanes), f32),
        scratch_shapes=[pltpu.SemaphoreType.DMA((rows,))],
        compiler_params=pltpu.CompilerParams(vmem_limit_bytes=52 * 2**20),
        cost_estimate=pl.CostEstimate(flops=0, bytes_accessed=4 * grouped.size, transcendentals=0),
        name="pack_other",
    )(core, grouped)


def prepare_kernel(core_ref, me_ref, grad_ref, places_ref, own_ref, index_ref, mine_ref, rows_ref, split, ordered, done):
    copies = row_copies(core_ref[0], grad_ref, own_ref, done)
    for copy in copies:
        copy.start()
    replicas, count, spans = places_ref.shape
    half = spans // 2
    source = lax.broadcasted_iota(jnp.int32, (spans, half), 0)
    target = lax.broadcasted_iota(jnp.int32, (spans, half), 1)
    places = places_ref[...].reshape(replicas * count, spans).astype(f32).astype(bf16)
    for parity in range(2):
        chooser = (source == 2 * target + parity).astype(f32).astype(bf16)
        chosen = jnp.dot(places, chooser, preferred_element_type=f32)
        split[:, parity * count : (parity + 1) * count, :] = chosen.reshape(replicas, count, half)
    mine_ref[...] = split[me_ref[0]]
    level = lax.broadcasted_iota(jnp.int32, (block, half), 0).astype(f32)
    for place, replica in enumerate(dp_order()):
        ordered[place] = split[replica]

    def row_of(places, parity, shift):
        rows = jnp.full(level.shape, (count * (1 - parity)) << shift, jnp.int32)
        for j in range(count):
            row = parity * count + j
            rows = jnp.where(places(row) == level, row << shift, rows)
        return rows

    for parity in range(2):
        at = slice(parity * block, (parity + 1) * block)
        rows_ref[at, :] = row_of(lambda row: mine_ref[row : row + 1, :], parity, 0)

    @pl.loop(0, replicas // 8)
    def _(word):
        for parity in range(2):
            packed = jnp.zeros(level.shape, jnp.int32)
            for field in range(8):
                place = word * 8 + field
                packed = packed | row_of(lambda row: ordered[place, row : row + 1, :], parity, 4 * field)
            index_ref[word, parity * block : (parity + 1) * block, :] = packed

    for copy in copies:
        copy.wait()


def prepare(core, me, grouped, positions):
    groups, tiles, places, _ = grouped.shape
    rows = groups * places // 2
    replicas, count, spans = positions.shape
    half = spans // 2
    return pl.pallas_call(
        prepare_kernel,
        in_specs=[smem, smem, anywhere, whole],
        out_specs=[whole] * 4,
        out_shape=[
            jax.ShapeDtypeStruct((rows, tiles, lanes), f32),
            jax.ShapeDtypeStruct((replicas // 8, 2 * block, half), jnp.int32),
            jax.ShapeDtypeStruct((2 * count, half), f32),
            jax.ShapeDtypeStruct((2 * block, half), jnp.int32),
        ],
        scratch_shapes=[
            pltpu.VMEM((replicas, 2 * count, half), f32),
            pltpu.VMEM((replicas, 2 * count, half), f32),
            pltpu.SemaphoreType.DMA((rows,)),
        ],
        compiler_params=narrow,
        cost_estimate=pl.CostEstimate(flops=9 * replicas * lanes * half, bytes_accessed=4 * grouped.size, transcendentals=0),
        name="prepare",
    )(core, me, grouped, positions)


def add_kernel(own_ref, arrived_ref, out_ref):
    for place, z in enumerate(z_order(out_ref.shape[0])):
        out_ref[place] = own_ref[z] + arrived_ref[z]


def add_step(own, arrived):
    return pl.pallas_call(
        add_kernel,
        in_specs=[whole, whole],
        out_specs=whole,
        out_shape=jax.ShapeDtypeStruct(own.shape, f32),
        compiler_params=params,
        cost_estimate=pl.CostEstimate(flops=own.size, bytes_accessed=12 * own.size, transcendentals=0),
        name="add_step",
    )(own, arrived)


def kept_kernel(parts_ref, moment_ref, places_ref, table_ref, copies_ref, own_ref, accumulated_ref):
    gradient = parts_ref[0]
    for source in range(1, parts_ref.shape[0]):
        gradient = gradient + parts_ref[source]
    accumulated = decay_rate * moment_ref[...] + gradient
    accumulated_ref[...] = accumulated
    coeffs = forward(accumulated, table_ref)
    level = lax.broadcasted_iota(jnp.int32, (block, coeffs.shape[1]), 0).astype(f32)
    own = places_ref[...]
    kept = []
    for parity in range(2):
        mine = coeffs[parity * block : (parity + 1) * block]
        for j in range(keep):
            row = parity * keep + j
            kept.append(jnp.sum(jnp.where(own[row : row + 1] == level, mine, 0.0), axis=0, keepdims=True))
    own_ref[...] = jnp.concatenate(kept, axis=0)
    copies_ref[...] = jnp.broadcast_to(own_ref[...][None], copies_ref.shape)


def kept_step(parts, moment, places, table, replicas):
    return pl.pallas_call(
        kept_kernel,
        in_specs=[whole] * 4,
        out_specs=[whole] * 3,
        out_shape=[
            jax.ShapeDtypeStruct((replicas,) + places.shape, f32),
            jax.ShapeDtypeStruct(places.shape, f32),
            jax.ShapeDtypeStruct(moment.shape, f32),
        ],
        compiler_params=params,
        cost_estimate=pl.CostEstimate(flops=6 * moment.size * lanes, bytes_accessed=4 * parts.size, transcendentals=0),
        name="kept_step",
    )(parts, moment, places, table)


def by_parity(values):
    even = lax.broadcasted_iota(jnp.int32, values.shape, 0) < keep
    return jnp.where(even, values, 0.0), jnp.where(even, 0.0, values)


def taken(values, rows):
    return jnp.take_along_axis(values, rows, axis=0, mode="promise_in_bounds")


def placed(values, word, shift):
    rows = lax.shift_right_logical(word, jnp.full(word.shape, shift, jnp.int32)) & 7
    return taken(values, rows)


def outputs_kernel(kept_ref, index_ref, own_ref, rows_ref, accumulated_ref, table_ref, update_ref, moment_ref, update, moment, done):
    replicas, _, half = kept_ref.shape
    chunks = range(0, 2 * block, 8)
    copies = []

    def send(source, target, at):
        copies.append(pltpu.make_async_copy(source.at[at], target.at[at], done.at[len(copies)]))
        copies[-1].start()

    sides = by_parity(own_ref[...])
    own = [taken(sides[k // block], rows_ref[k : k + 8, :]) for k in chunks]
    moment[...] = accumulated_ref[...] - inverse(jnp.concatenate(own, axis=0), table_ref).T
    send(moment, moment_ref, slice(0, half))
    for first in range(0, half, lanes):
        at = slice(first, min(first + lanes, half))
        sums = [jnp.zeros((8, at.stop - first), f32) for _ in chunks]
        for replica in range(replicas):
            sides = by_parity(kept_ref[replica, :, at])
            sums = [
                total + placed(sides[k // block], index_ref[replica // 8, k : k + 8, at], replica % 8 * 4)
                for k, total in zip(chunks, sums)
            ]
        mean = jnp.concatenate(sums, axis=0) * (1.0 / replicas)
        averaged = inverse(mean, table_ref)
        parts = []
        for side in (slice(0, block), slice(block, 2 * block)):
            meansq = jnp.sum(mean[side] * mean[side], axis=0, keepdims=True) * (1.0 / block)
            parts.append(averaged[side] * lax.rsqrt(averaged[side] * averaged[side] + (meansq + epsilon)))
        update[at, :] = jnp.concatenate(parts, axis=0).T
        send(update, update_ref, at)
    for copy in copies:
        copy.wait()


def outputs_step(kept, index, own, rows, accumulated, table):
    replicas, _, half = kept.shape
    return pl.pallas_call(
        outputs_kernel,
        in_specs=[whole] * 6,
        out_specs=[anywhere] * 2,
        out_shape=[jax.ShapeDtypeStruct(accumulated.shape, f32)] * 2,
        scratch_shapes=[
            pltpu.VMEM(accumulated.shape, f32),
            pltpu.VMEM(accumulated.shape, f32),
            pltpu.SemaphoreType.DMA((1 + pl.cdiv(half, lanes),)),
        ],
        compiler_params=params,
        cost_estimate=pl.CostEstimate(flops=9 * replicas * lanes * half, bytes_accessed=8 * kept.size, transcendentals=lanes * half),
        name="outputs_step",
    )(kept, index, own, rows, accumulated, table)


def body(grad_parts, momentum, positions):
    columns = momentum.shape[-1]
    tiles = columns // lanes
    devices = lax.axis_size("fsdp")
    me = lax.axis_index("fsdp")
    core = (me % 2).reshape(1)
    rows = grad_parts.shape[2]
    grouped = grad_parts[0, 0].reshape(rows // 8, 8, tiles, lanes).transpose(0, 2, 1, 3)
    positions = positions[:, 0]
    forward_table, inverse_table = (jnp.asarray(table) for table in tables())
    replica = lax.axis_index("dp").reshape(1)
    arrived = lax.ppermute(pack_other(grouped, core), "fsdp", [(i, i ^ 1) for i in range(devices)])
    own, index, places, rows = prepare(core, replica, grouped, positions)
    own, index, places, rows, arrived = lax.optimization_barrier((own, index, places, rows, arrived))
    groups = [[2 * z + side for z in z_order(devices // 2)] for side in range(2)]
    parts = lax.all_to_all(add_step(own, arrived), "fsdp", 0, 0, tiled=True, axis_index_groups=groups)
    copies, kept, accumulated = kept_step(parts, momentum.reshape(tiles, lanes), places, forward_table, positions.shape[0])
    everyone = lax.all_to_all(copies, "dp", 0, 0, tiled=True, axis_index_groups=[dp_order()])
    update, new_moment = outputs_step(everyone, index, kept, rows, accumulated, inverse_table)
    return update.reshape(1, columns), new_moment.reshape(1, 1, columns)


def solution(mesh):
    in_specs = (P("dp", "fsdp", None, None), P("dp", "fsdp", None), P(None, "fsdp", None, None))
    out_specs = (P("fsdp", None), P("dp", "fsdp", None))
    return jax.shard_map(body, mesh=mesh, in_specs=in_specs, out_specs=out_specs, check_vma=False)
```

```python
import functools

import jax
import jax.numpy as jnp
import numpy as np
from jax import lax
from jax.experimental import pallas as pl
from jax.experimental.pallas import tpu as pltpu
from jax.sharding import PartitionSpec as P

decay_rate = 0.999
epsilon = 1e-06
block = 64
lanes = 128
keep = 4
f32, bf16 = jnp.float32, jnp.bfloat16
whole = pl.BlockSpec(memory_space=pltpu.VMEM)
smem = pl.BlockSpec(memory_space=pltpu.SMEM)
anywhere = pl.BlockSpec(memory_space=pl.ANY)
params = pltpu.CompilerParams(vmem_limit_bytes=12 * 2**20)
narrow = pltpu.CompilerParams(vmem_limit_bytes=51 * 2**20)


def z_order(count):
    return list(range(count - 1, -1, -1))


def dp_order():
    lag_x, lag_y = (0, 6, 9, 13), (0, 4, 12, 18, 31, 26, 24, 23)
    lag = [x + y for x in lag_x for y in lag_y]
    return sorted(range(len(lag)), key=lambda replica: (lag[replica], replica), reverse=True)


def paired_table():
    frequency = np.arange(block)[:, None]
    sample = np.arange(block)[None, :]
    cosines = np.cos(np.pi * (2.0 * sample + 1.0) * frequency / (2.0 * block))
    norming = np.where(frequency == 0, np.sqrt(1.0 / block), np.sqrt(2.0 / block))
    return np.kron(np.eye(2), cosines * norming).astype(np.float32)


def tables():
    table = paired_table()
    high = table.astype(jnp.bfloat16)
    low = (table - high.astype(np.float32)).astype(jnp.bfloat16)
    none = np.zeros_like(high)
    return np.block([[high, high], [low, none]]), np.block([[high.T, high.T], [low.T, none]])


def halves(x):
    high = x.astype(bf16)
    return high, (x - high.astype(f32)).astype(bf16)


def forward(fields, table_ref):
    parts = jnp.concatenate(halves(fields), axis=1)
    both = lax.dot_general(table_ref[...], parts, (((1,), (1,)), ((), ())), preferred_element_type=f32)
    return both[:lanes] + both[lanes:]


def inverse(coeffs, table_ref):
    parts = jnp.concatenate(halves(coeffs), axis=0)
    both = jnp.dot(table_ref[...], parts, preferred_element_type=f32)
    return both[:lanes] + both[lanes:]


def row_copies(core, grad_ref, out_ref, done):
    places = grad_ref.shape[2] // 2
    return [
        pltpu.make_async_copy(
            grad_ref.at[z // places, :, 2 * (z % places) + core, :], out_ref.at[z], done.at[z]
        )
        for z in range(out_ref.shape[0])
    ]


def pack_kernel(core_ref, grad_ref, out_ref, done):
    copies = row_copies(1 - core_ref[0], grad_ref, out_ref, done)
    for copy in copies:
        copy.start()
    for copy in copies:
        copy.wait()


def pack_other(grouped, core):
    groups, tiles, places, _ = grouped.shape
    rows = groups * places // 2
    return pl.pallas_call(
        pack_kernel,
        in_specs=[smem, anywhere],
        out_specs=whole,
        out_shape=jax.ShapeDtypeStruct((rows, tiles, lanes), f32),
        scratch_shapes=[pltpu.SemaphoreType.DMA((rows,))],
        compiler_params=pltpu.CompilerParams(vmem_limit_bytes=52 * 2**20),
        cost_estimate=pl.CostEstimate(flops=0, bytes_accessed=4 * grouped.size, transcendentals=0),
        name="pack_other",
    )(core, grouped)


def prepare_kernel(core_ref, me_ref, grad_ref, places_ref, own_ref, index_ref, mine_ref, rows_ref, split, ordered, done):
    copies = row_copies(core_ref[0], grad_ref, own_ref, done)
    for copy in copies:
        copy.start()
    replicas, count, spans = places_ref.shape
    half = spans // 2
    source = lax.broadcasted_iota(jnp.int32, (spans, half), 0)
    target = lax.broadcasted_iota(jnp.int32, (spans, half), 1)
    places = places_ref[...].reshape(replicas * count, spans).astype(f32).astype(bf16)
    for parity in range(2):
        chooser = (source == 2 * target + parity).astype(f32).astype(bf16)
        chosen = jnp.dot(places, chooser, preferred_element_type=f32)
        split[:, parity * count : (parity + 1) * count, :] = chosen.reshape(replicas, count, half)
    mine_ref[...] = split[me_ref[0]]
    level = lax.broadcasted_iota(jnp.int32, (block, half), 0).astype(f32)
    for place, replica in enumerate(dp_order()):
        ordered[place] = split[replica]

    def row_of(places, parity, shift):
        rows = jnp.full(level.shape, (count * (1 - parity)) << shift, jnp.int32)
        for j in range(count):
            row = parity * count + j
            rows = jnp.where(places(row) == level, row << shift, rows)
        return rows

    for parity in range(2):
        at = slice(parity * block, (parity + 1) * block)
        rows_ref[at, :] = row_of(lambda row: mine_ref[row : row + 1, :], parity, 0)

    @pl.loop(0, replicas // 8)
    def _(word):
        for parity in range(2):
            packed = jnp.zeros(level.shape, jnp.int32)
            for field in range(8):
                place = word * 8 + field
                packed = packed | row_of(lambda row: ordered[place, row : row + 1, :], parity, 4 * field)
            index_ref[word, parity * block : (parity + 1) * block, :] = packed

    for copy in copies:
        copy.wait()


def prepare(core, me, grouped, positions):
    groups, tiles, places, _ = grouped.shape
    rows = groups * places // 2
    replicas, count, spans = positions.shape
    half = spans // 2
    return pl.pallas_call(
        prepare_kernel,
        in_specs=[smem, smem, anywhere, whole],
        out_specs=[whole] * 4,
        out_shape=[
            jax.ShapeDtypeStruct((rows, tiles, lanes), f32),
            jax.ShapeDtypeStruct((replicas // 8, 2 * block, half), jnp.int32),
            jax.ShapeDtypeStruct((2 * count, half), f32),
            jax.ShapeDtypeStruct((2 * block, half), jnp.int32),
        ],
        scratch_shapes=[
            pltpu.VMEM((replicas, 2 * count, half), f32),
            pltpu.VMEM((replicas, 2 * count, half), f32),
            pltpu.SemaphoreType.DMA((rows,)),
        ],
        compiler_params=narrow,
        cost_estimate=pl.CostEstimate(flops=9 * replicas * lanes * half, bytes_accessed=4 * grouped.size, transcendentals=0),
        name="prepare",
    )(core, me, grouped, positions)


def add_kernel(own_ref, arrived_ref, out_ref):
    for place, z in enumerate(z_order(out_ref.shape[0])):
        out_ref[place] = own_ref[z] + arrived_ref[z]


def add_step(own, arrived):
    return pl.pallas_call(
        add_kernel,
        in_specs=[whole, whole],
        out_specs=whole,
        out_shape=jax.ShapeDtypeStruct(own.shape, f32),
        compiler_params=params,
        cost_estimate=pl.CostEstimate(flops=own.size, bytes_accessed=12 * own.size, transcendentals=0),
        name="add_step",
    )(own, arrived)


def kept_kernel(parts_ref, moment_ref, places_ref, table_ref, copies_ref, own_ref, accumulated_ref):
    gradient = parts_ref[0]
    for source in range(1, parts_ref.shape[0]):
        gradient = gradient + parts_ref[source]
    accumulated = decay_rate * moment_ref[...] + gradient
    accumulated_ref[...] = accumulated
    coeffs = forward(accumulated, table_ref)
    level = lax.broadcasted_iota(jnp.int32, (block, coeffs.shape[1]), 0).astype(f32)
    own = places_ref[...]
    kept = []
    for parity in range(2):
        mine = coeffs[parity * block : (parity + 1) * block]
        for j in range(keep):
            row = parity * keep + j
            kept.append(jnp.sum(jnp.where(own[row : row + 1] == level, mine, 0.0), axis=0, keepdims=True))
    own_ref[...] = jnp.concatenate(kept, axis=0)
    copies_ref[...] = jnp.broadcast_to(own_ref[...][None], copies_ref.shape)


def kept_step(parts, moment, places, table, replicas):
    return pl.pallas_call(
        kept_kernel,
        in_specs=[whole] * 4,
        out_specs=[whole] * 3,
        out_shape=[
            jax.ShapeDtypeStruct((replicas,) + places.shape, f32),
            jax.ShapeDtypeStruct(places.shape, f32),
            jax.ShapeDtypeStruct(moment.shape, f32),
        ],
        compiler_params=params,
        cost_estimate=pl.CostEstimate(flops=6 * moment.size * lanes, bytes_accessed=4 * parts.size, transcendentals=0),
        name="kept_step",
    )(parts, moment, places, table)


def by_parity(values):
    even = lax.broadcasted_iota(jnp.int32, values.shape, 0) < keep
    return jnp.where(even, values, 0.0), jnp.where(even, 0.0, values)


def taken(values, rows):
    return jnp.take_along_axis(values, rows, axis=0, mode="promise_in_bounds")


def placed(values, word, shift):
    rows = lax.shift_right_logical(word, jnp.full(word.shape, shift, jnp.int32)) & 7
    return taken(values, rows)


def outputs_kernel(kept_ref, index_ref, own_ref, rows_ref, accumulated_ref, table_ref, update_ref, moment_ref, update, moment, done):
    replicas, _, half = kept_ref.shape
    chunks = range(0, 2 * block, 8)
    copies = []

    def send(source, target, at):
        copies.append(pltpu.make_async_copy(source.at[at], target.at[at], done.at[len(copies)]))
        copies[-1].start()

    sides = by_parity(own_ref[...])
    own = [taken(sides[k // block], rows_ref[k : k + 8, :]) for k in chunks]
    moment[...] = accumulated_ref[...] - inverse(jnp.concatenate(own, axis=0), table_ref).T
    send(moment, moment_ref, slice(0, half))
    for first in range(0, half, lanes):
        at = slice(first, min(first + lanes, half))
        sums = [jnp.zeros((8, at.stop - first), f32) for _ in chunks]
        for replica in range(replicas):
            sides = by_parity(kept_ref[replica, :, at])
            sums = [
                total + placed(sides[k // block], index_ref[replica // 8, k : k + 8, at], replica % 8 * 4)
                for k, total in zip(chunks, sums)
            ]
        mean = jnp.concatenate(sums, axis=0) * (1.0 / replicas)
        averaged = inverse(mean, table_ref)
        parts = []
        for side in (slice(0, block), slice(block, 2 * block)):
            meansq = jnp.sum(mean[side] * mean[side], axis=0, keepdims=True) * (1.0 / block)
            parts.append(averaged[side] * lax.rsqrt(averaged[side] * averaged[side] + (meansq + epsilon)))
        update[at, :] = jnp.concatenate(parts, axis=0).T
        send(update, update_ref, at)
    for copy in copies:
        copy.wait()


def outputs_step(kept, index, own, rows, accumulated, table):
    replicas, _, half = kept.shape
    return pl.pallas_call(
        outputs_kernel,
        in_specs=[whole] * 6,
        out_specs=[anywhere] * 2,
        out_shape=[jax.ShapeDtypeStruct(accumulated.shape, f32)] * 2,
        scratch_shapes=[
            pltpu.VMEM(accumulated.shape, f32),
            pltpu.VMEM(accumulated.shape, f32),
            pltpu.SemaphoreType.DMA((1 + pl.cdiv(half, lanes),)),
        ],
        compiler_params=params,
        cost_estimate=pl.CostEstimate(flops=9 * replicas * lanes * half, bytes_accessed=8 * kept.size, transcendentals=lanes * half),
        name="outputs_step",
    )(kept, index, own, rows, accumulated, table)


def body(grad_parts, momentum, positions):
    columns = momentum.shape[-1]
    tiles = columns // lanes
    devices = lax.axis_size("fsdp")
    me = lax.axis_index("fsdp")
    core = (me % 2).reshape(1)
    rows = grad_parts.shape[2]
    grouped = grad_parts[0, 0].reshape(rows // 8, 8, tiles, lanes).transpose(0, 2, 1, 3)
    positions = positions[:, 0]
    forward_table, inverse_table = (jnp.asarray(table) for table in tables())
    replica = lax.axis_index("dp").reshape(1)
    arrived = lax.ppermute(pack_other(grouped, core), "fsdp", [(i, i ^ 1) for i in range(devices)])
    own, index, places, rows = prepare(core, replica, grouped, positions)
    own, index, places, rows, arrived = lax.optimization_barrier((own, index, places, rows, arrived))
    groups = [[2 * z + side for z in z_order(devices // 2)] for side in range(2)]
    parts = lax.all_to_all(add_step(own, arrived), "fsdp", 0, 0, tiled=True, axis_index_groups=groups)
    copies, kept, accumulated = kept_step(parts, momentum.reshape(tiles, lanes), places, forward_table, positions.shape[0])
    everyone = lax.all_to_all(copies, "dp", 0, 0, tiled=True, axis_index_groups=[dp_order()])
    update, new_moment = outputs_step(everyone, index, kept, rows, accumulated, inverse_table)
    return update.reshape(1, columns), new_moment.reshape(1, 1, columns)


def solution(mesh):
    in_specs = (P("dp", "fsdp", None, None), P("dp", "fsdp", None), P(None, "fsdp", None, None))
    out_specs = (P("fsdp", None), P("dp", "fsdp", None))
    return jax.shard_map(body, mesh=mesh, in_specs=in_specs, out_specs=out_specs, check_vma=False)
```

```python
import functools

import jax
import jax.numpy as jnp
import numpy as np
from jax import lax
from jax.experimental import pallas as pl
from jax.experimental.pallas import tpu as pltpu
from jax.sharding import PartitionSpec as P

decay_rate = 0.999
epsilon = 1e-06
block = 64
lanes = 128
keep = 4
f32, bf16 = jnp.float32, jnp.bfloat16
whole = pl.BlockSpec(memory_space=pltpu.VMEM)
smem = pl.BlockSpec(memory_space=pltpu.SMEM)
anywhere = pl.BlockSpec(memory_space=pl.ANY)
params = pltpu.CompilerParams(vmem_limit_bytes=12 * 2**20)
narrow = pltpu.CompilerParams(vmem_limit_bytes=51 * 2**20)


def z_order(count):
    return list(range(count - 1, -1, -2)) + list(range(count - 2, -1, -2))


def dp_order():
    lag_x, lag_y = (0, 6, 9, 13), (0, 4, 12, 18, 31, 26, 24, 23)
    lag = [x + y for x in lag_x for y in lag_y]
    return sorted(range(len(lag)), key=lambda replica: (lag[replica], replica), reverse=True)


def paired_table():
    frequency = np.arange(block)[:, None]
    sample = np.arange(block)[None, :]
    cosines = np.cos(np.pi * (2.0 * sample + 1.0) * frequency / (2.0 * block))
    norming = np.where(frequency == 0, np.sqrt(1.0 / block), np.sqrt(2.0 / block))
    return np.kron(np.eye(2), cosines * norming).astype(np.float32)


def tables():
    table = paired_table()
    high = table.astype(jnp.bfloat16)
    low = (table - high.astype(np.float32)).astype(jnp.bfloat16)
    none = np.zeros_like(high)
    return np.block([[high, high], [low, none]]), np.block([[high.T, high.T], [low.T, none]])


def halves(x):
    high = x.astype(bf16)
    return high, (x - high.astype(f32)).astype(bf16)


def forward(fields, table_ref):
    parts = jnp.concatenate(halves(fields), axis=1)
    both = lax.dot_general(table_ref[...], parts, (((1,), (1,)), ((), ())), preferred_element_type=f32)
    return both[:lanes] + both[lanes:]


def inverse(coeffs, table_ref):
    parts = jnp.concatenate(halves(coeffs), axis=0)
    both = jnp.dot(table_ref[...], parts, preferred_element_type=f32)
    return both[:lanes] + both[lanes:]


def row_copies(core, grad_ref, out_ref, done):
    places = grad_ref.shape[2] // 2
    return [
        pltpu.make_async_copy(
            grad_ref.at[z // places, :, 2 * (z % places) + core, :], out_ref.at[z], done.at[z]
        )
        for z in range(out_ref.shape[0])
    ]


def pack_kernel(core_ref, grad_ref, out_ref, done):
    copies = row_copies(1 - core_ref[0], grad_ref, out_ref, done)
    for copy in copies:
        copy.start()
    for copy in copies:
        copy.wait()


def pack_other(grouped, core):
    groups, tiles, places, _ = grouped.shape
    rows = groups * places // 2
    return pl.pallas_call(
        pack_kernel,
        in_specs=[smem, anywhere],
        out_specs=whole,
        out_shape=jax.ShapeDtypeStruct((rows, tiles, lanes), f32),
        scratch_shapes=[pltpu.SemaphoreType.DMA((rows,))],
        compiler_params=pltpu.CompilerParams(vmem_limit_bytes=52 * 2**20),
        cost_estimate=pl.CostEstimate(flops=0, bytes_accessed=4 * grouped.size, transcendentals=0),
        name="pack_other",
    )(core, grouped)


def prepare_kernel(core_ref, me_ref, grad_ref, places_ref, own_ref, index_ref, mine_ref, rows_ref, split, ordered, done):
    copies = row_copies(core_ref[0], grad_ref, own_ref, done)
    for copy in copies:
        copy.start()
    replicas, count, spans = places_ref.shape
    half = spans // 2
    source = lax.broadcasted_iota(jnp.int32, (spans, half), 0)
    target = lax.broadcasted_iota(jnp.int32, (spans, half), 1)
    places = places_ref[...].reshape(replicas * count, spans).astype(f32).astype(bf16)
    for parity in range(2):
        chooser = (source == 2 * target + parity).astype(f32).astype(bf16)
        chosen = jnp.dot(places, chooser, preferred_element_type=f32)
        split[:, parity * count : (parity + 1) * count, :] = chosen.reshape(replicas, count, half)
    mine_ref[...] = split[me_ref[0]]
    level = lax.broadcasted_iota(jnp.int32, (block, half), 0).astype(f32)
    for place, replica in enumerate(dp_order()):
        ordered[place] = split[replica]

    def row_of(places, parity, shift):
        rows = jnp.full(level.shape, (count * (1 - parity)) << shift, jnp.int32)
        for j in range(count):
            row = parity * count + j
            rows = jnp.where(places(row) == level, row << shift, rows)
        return rows

    for parity in range(2):
        at = slice(parity * block, (parity + 1) * block)
        rows_ref[at, :] = row_of(lambda row: mine_ref[row : row + 1, :], parity, 0)

    @pl.loop(0, replicas // 8)
    def _(word):
        for parity in range(2):
            packed = jnp.zeros(level.shape, jnp.int32)
            for field in range(8):
                place = word * 8 + field
                packed = packed | row_of(lambda row: ordered[place, row : row + 1, :], parity, 4 * field)
            index_ref[word, parity * block : (parity + 1) * block, :] = packed

    for copy in copies:
        copy.wait()


def prepare(core, me, grouped, positions):
    groups, tiles, places, _ = grouped.shape
    rows = groups * places // 2
    replicas, count, spans = positions.shape
    half = spans // 2
    return pl.pallas_call(
        prepare_kernel,
        in_specs=[smem, smem, anywhere, whole],
        out_specs=[whole] * 4,
        out_shape=[
            jax.ShapeDtypeStruct((rows, tiles, lanes), f32),
            jax.ShapeDtypeStruct((replicas // 8, 2 * block, half), jnp.int32),
            jax.ShapeDtypeStruct((2 * count, half), f32),
            jax.ShapeDtypeStruct((2 * block, half), jnp.int32),
        ],
        scratch_shapes=[
            pltpu.VMEM((replicas, 2 * count, half), f32),
            pltpu.VMEM((replicas, 2 * count, half), f32),
            pltpu.SemaphoreType.DMA((rows,)),
        ],
        compiler_params=narrow,
        cost_estimate=pl.CostEstimate(flops=9 * replicas * lanes * half, bytes_accessed=4 * grouped.size, transcendentals=0),
        name="prepare",
    )(core, me, grouped, positions)


def add_kernel(own_ref, arrived_ref, out_ref):
    for place, z in enumerate(z_order(out_ref.shape[0])):
        out_ref[place] = own_ref[z] + arrived_ref[z]


def add_step(own, arrived):
    return pl.pallas_call(
        add_kernel,
        in_specs=[whole, whole],
        out_specs=whole,
        out_shape=jax.ShapeDtypeStruct(own.shape, f32),
        compiler_params=params,
        cost_estimate=pl.CostEstimate(flops=own.size, bytes_accessed=12 * own.size, transcendentals=0),
        name="add_step",
    )(own, arrived)


def kept_kernel(parts_ref, moment_ref, places_ref, table_ref, copies_ref, own_ref, accumulated_ref):
    gradient = parts_ref[0]
    for source in range(1, parts_ref.shape[0]):
        gradient = gradient + parts_ref[source]
    accumulated = decay_rate * moment_ref[...] + gradient
    accumulated_ref[...] = accumulated
    coeffs = forward(accumulated, table_ref)
    level = lax.broadcasted_iota(jnp.int32, (block, coeffs.shape[1]), 0).astype(f32)
    own = places_ref[...]
    kept = []
    for parity in range(2):
        mine = coeffs[parity * block : (parity + 1) * block]
        for j in range(keep):
            row = parity * keep + j
            kept.append(jnp.sum(jnp.where(own[row : row + 1] == level, mine, 0.0), axis=0, keepdims=True))
    own_ref[...] = jnp.concatenate(kept, axis=0)
    copies_ref[...] = jnp.broadcast_to(own_ref[...][None], copies_ref.shape)


def kept_step(parts, moment, places, table, replicas):
    return pl.pallas_call(
        kept_kernel,
        in_specs=[whole] * 4,
        out_specs=[whole] * 3,
        out_shape=[
            jax.ShapeDtypeStruct((replicas,) + places.shape, f32),
            jax.ShapeDtypeStruct(places.shape, f32),
            jax.ShapeDtypeStruct(moment.shape, f32),
        ],
        compiler_params=params,
        cost_estimate=pl.CostEstimate(flops=6 * moment.size * lanes, bytes_accessed=4 * parts.size, transcendentals=0),
        name="kept_step",
    )(parts, moment, places, table)


def by_parity(values):
    even = lax.broadcasted_iota(jnp.int32, values.shape, 0) < keep
    return jnp.where(even, values, 0.0), jnp.where(even, 0.0, values)


def taken(values, rows):
    return jnp.take_along_axis(values, rows, axis=0, mode="promise_in_bounds")


def placed(values, word, shift):
    rows = lax.shift_right_logical(word, jnp.full(word.shape, shift, jnp.int32)) & 7
    return taken(values, rows)


def outputs_kernel(kept_ref, index_ref, own_ref, rows_ref, accumulated_ref, table_ref, update_ref, moment_ref, update, moment, done):
    replicas, _, half = kept_ref.shape
    chunks = range(0, 2 * block, 8)
    copies = []

    def send(source, target, at):
        copies.append(pltpu.make_async_copy(source.at[at], target.at[at], done.at[len(copies)]))
        copies[-1].start()

    sides = by_parity(own_ref[...])
    own = [taken(sides[k // block], rows_ref[k : k + 8, :]) for k in chunks]
    moment[...] = accumulated_ref[...] - inverse(jnp.concatenate(own, axis=0), table_ref).T
    send(moment, moment_ref, slice(0, half))
    for first in range(0, half, lanes):
        at = slice(first, min(first + lanes, half))
        sums = [jnp.zeros((8, at.stop - first), f32) for _ in chunks]
        for replica in range(replicas):
            sides = by_parity(kept_ref[replica, :, at])
            sums = [
                total + placed(sides[k // block], index_ref[replica // 8, k : k + 8, at], replica % 8 * 4)
                for k, total in zip(chunks, sums)
            ]
        mean = jnp.concatenate(sums, axis=0) * (1.0 / replicas)
        averaged = inverse(mean, table_ref)
        parts = []
        for side in (slice(0, block), slice(block, 2 * block)):
            meansq = jnp.sum(mean[side] * mean[side], axis=0, keepdims=True) * (1.0 / block)
            parts.append(averaged[side] * lax.rsqrt(averaged[side] * averaged[side] + (meansq + epsilon)))
        update[at, :] = jnp.concatenate(parts, axis=0).T
        send(update, update_ref, at)
    for copy in copies:
        copy.wait()


def outputs_step(kept, index, own, rows, accumulated, table):
    replicas, _, half = kept.shape
    return pl.pallas_call(
        outputs_kernel,
        in_specs=[whole] * 6,
        out_specs=[anywhere] * 2,
        out_shape=[jax.ShapeDtypeStruct(accumulated.shape, f32)] * 2,
        scratch_shapes=[
            pltpu.VMEM(accumulated.shape, f32),
            pltpu.VMEM(accumulated.shape, f32),
            pltpu.SemaphoreType.DMA((1 + pl.cdiv(half, lanes),)),
        ],
        compiler_params=params,
        cost_estimate=pl.CostEstimate(flops=9 * replicas * lanes * half, bytes_accessed=8 * kept.size, transcendentals=lanes * half),
        name="outputs_step",
    )(kept, index, own, rows, accumulated, table)


def body(grad_parts, momentum, positions):
    columns = momentum.shape[-1]
    tiles = columns // lanes
    devices = lax.axis_size("fsdp")
    me = lax.axis_index("fsdp")
    core = (me % 2).reshape(1)
    rows = grad_parts.shape[2]
    grouped = grad_parts[0, 0].reshape(rows // 8, 8, tiles, lanes).transpose(0, 2, 1, 3)
    positions = positions[:, 0]
    forward_table, inverse_table = (jnp.asarray(table) for table in tables())
    replica = lax.axis_index("dp").reshape(1)
    arrived = lax.ppermute(pack_other(grouped, core), "fsdp", [(i, i ^ 1) for i in range(devices)])
    own, index, places, rows = prepare(core, replica, grouped, positions)
    own, index, places, rows, arrived = lax.optimization_barrier((own, index, places, rows, arrived))
    groups = [[2 * z + side for z in z_order(devices // 2)] for side in range(2)]
    parts = lax.all_to_all(add_step(own, arrived), "fsdp", 0, 0, tiled=True, axis_index_groups=groups)
    copies, kept, accumulated = kept_step(parts, momentum.reshape(tiles, lanes), places, forward_table, positions.shape[0])
    everyone = lax.all_to_all(copies, "dp", 0, 0, tiled=True, axis_index_groups=[dp_order()])
    update, new_moment = outputs_step(everyone, index, kept, rows, accumulated, inverse_table)
    return update.reshape(1, columns), new_moment.reshape(1, 1, columns)


def solution(mesh):
    in_specs = (P("dp", "fsdp", None, None), P("dp", "fsdp", None), P(None, "fsdp", None, None))
    out_specs = (P("fsdp", None), P("dp", "fsdp", None))
    return jax.shard_map(body, mesh=mesh, in_specs=in_specs, out_specs=out_specs, check_vma=False)
```
